32 devices in a mesh: row: 4 (over y, x), col: 8 (over z, core).
Axes of the slice: x: 2, y: 2, z: 4, core: 2. Of those that a mesh axis runs over, the one named last changes fastest.
Arguments:
- samples: float32 [1024, 64, 128], P(('row', 'col')), may hold values from -6 to 6
- omega: float32 [4, 8, 128, 128, 128], P('row', 'col'), may hold values from -0.12 to 2.12
- block_rows: int32 [4, 8, 128], P('row', 'col'), may hold values from -1 to 1023, as said below
- block_cols: int32 [4, 8, 128], P('row', 'col'), may hold values from -1 to 1023, as said below
Outputs:
- omega_next: float32 [4, 8, 128, 128, 128], P('row', 'col')
The draws below stay inside these ranges and needn't reach their ends.
Inputs may be any that keep to these rules, and one draw needn't show every extreme that they name: `block_rows`: slots 0 to 31 of the device at (a, b) hold the diagonal blocks I = J = (a * 8 + b) * 32 + k in order of k; the other slots hold distinct off-diagonal blocks whose block row lies in a * 1024 / 4 up to (a + 1) * 1024 / 4 - 1 and whose block column J has (J // 32) % 8 = b; live slots come first and -1 fills the rest; some device has all 128 slots live. `block_cols`: -1 exactly where block_rows is -1.
All inputs are finite; a program needn't handle non-finite values.
Results may differ from the reference program's by a relative error of at most 0.0003.
Values sent between devices are 32-bit elements; how exact they have to be, the bound alone decides.
No kernel may reach another device: no remote copies, remote signals or barrier semaphores. Data moves between devices by JAX's collectives and lax.ppermute only.
A program may use at most 128 MiB of HBM per device.

```python
import jax
import jax.numpy as jnp
from jax import lax

BS = 128
N_SAMP = 64
OFF_MOST = 96
ITERS = 2
NB = 1024
BPS = 32
CAP = 128
N_ROW = 4
N_COL = 8


def pattern_lists(key):
    pattern_key = jax.random.fold_in(key, 7)
    first_key, second_key, top_key, pick_key = jax.random.split(pattern_key, 4)
    devices_all = N_ROW * N_COL
    group_rows = NB // N_ROW
    group_cols = NB // N_COL
    factor_one = jax.random.randint(first_key, (devices_all,), 1, OFF_MOST + 1)
    factor_two = jax.random.randint(second_key, (devices_all,), 1, OFF_MOST + 1)
    active_counts = (factor_one * factor_two + OFF_MOST - 1) // OFF_MOST
    busiest = jax.random.randint(top_key, (), 0, devices_all)
    active_counts = jnp.where(jnp.arange(devices_all) == busiest, OFF_MOST, active_counts)

    def one_device(device, active_count):
        row_group = device // N_COL
        col_group = device % N_COL
        shuffled = jax.random.permutation(jax.random.fold_in(pick_key, device), group_rows * group_cols)
        local_row = shuffled // group_cols
        local_col = shuffled % group_cols
        global_row = row_group * group_rows + local_row
        global_col = (local_col // BPS * N_COL + col_group) * BPS + local_col % BPS
        is_diag = (global_row == global_col).astype(jnp.int32)
        ranked = jnp.argsort(is_diag, stable=True)[:OFF_MOST]
        kept_mask = jnp.arange(OFF_MOST) < active_count
        off_rows = jnp.where(kept_mask, global_row[ranked], -1)
        off_cols = jnp.where(kept_mask, global_col[ranked], -1)
        diag_ids = (row_group * N_COL + col_group) * BPS + jnp.arange(BPS)
        return (jnp.concatenate([diag_ids, off_rows]), jnp.concatenate([diag_ids, off_cols]))
    row_table, col_table = jax.vmap(one_device)(jnp.arange(devices_all), active_counts)
    row_table = row_table.reshape(N_ROW, N_COL, CAP).astype(jnp.int32)
    col_table = col_table.reshape(N_ROW, N_COL, CAP).astype(jnp.int32)
    return (row_table, col_table)


def draw_block_rows(key, part):
    return pattern_lists(key)[0]


def draw_block_cols(key, part):
    return pattern_lists(key)[1]


def draw_omega(key, part):
    noise_key, gain_key = jax.random.split(jax.random.fold_in(key, 11))
    full_shape = (N_ROW, N_COL, CAP, BS, BS)
    noise_part = 0.03 * jax.random.truncated_normal(noise_key, -4.0, 4.0, full_shape, jnp.float32)
    gain_values = jax.random.uniform(gain_key, (N_ROW, N_COL, CAP, BS), jnp.float32, 1.0, 2.0)
    diag_slot = (jnp.arange(CAP) < BPS).astype(jnp.float32)
    identity = jnp.eye(BS, dtype=jnp.float32)
    return noise_part + diag_slot[:, None, None] * gain_values[..., None] * identity


def level_of(own_key, extent, cuts, smallest, high):
    level = 1.0
    for axis_at, shards_of in cuts:
        heights = jax.random.uniform(jax.random.fold_in(jax.random.fold_in(own_key, 6), axis_at), (shards_of,), jnp.float32, smallest / len(cuts), high / len(cuts))
        level = level * jnp.repeat(jnp.exp(heights), extent[axis_at] // shards_of).reshape((-1,) + (1,) * (len(extent) - 1 - axis_at))
    return level


def normal_values(key, dims, scale, most, pieces=(), kind=jnp.bfloat16):
    drawn = scale * jax.random.normal(key, dims, jnp.float32)
    if pieces:
        drawn = drawn * level_of(key, dims, pieces, -0.22, 0.18)
    return jnp.clip(drawn, -most, most).astype(kind)


def setup_inputs(seed: int = 0) -> dict:
    key_of = jax.random.split(jax.random.key(seed), 5)
    return {
        "samples": normal_values(key_of[0], (NB, N_SAMP, BS), 1.0, 6.0, ((0, 32),), jnp.float32),
        "omega": draw_omega(jax.random.fold_in(key_of[4], 71), 0),
        "block_rows": draw_block_rows(jax.random.fold_in(key_of[4], 71), 0),
        "block_cols": draw_block_cols(jax.random.fold_in(key_of[4], 71), 0),
    }


STEP = 0.5
PENALTY = 0.1

def gradient_blocks(left_totals, right_samples, left_samples, right_totals, sample_count):
    forward = jnp.einsum('snb,snk->sbk', left_totals, right_samples, precision=lax.Precision.HIGHEST)
    mirrored = jnp.einsum('snb,snk->sbk', left_samples, right_totals, precision=lax.Precision.HIGHEST)
    return (forward + mirrored) * (0.5 / sample_count)

def proximal(current, grad, active, on_diagonal):
    stepped = current - STEP * grad
    eye_mask = jnp.eye(current.shape[-1], dtype=bool)[None] & on_diagonal[:, None, None]
    shrunk = jnp.sign(stepped) * jnp.maximum(jnp.abs(stepped) - STEP * PENALTY, 0.0)
    lifted = 0.5 * (stepped + jnp.sqrt(stepped * stepped + 4.0 * STEP))
    updated = jnp.where(eye_mask, lifted, shrunk)
    return jnp.where(active[:, None, None], updated, 0.0)

def reference(samples, omega, block_rows, block_cols):
    total_blocks = samples.shape[0]
    sample_count = samples.shape[1]
    width = samples.shape[2]
    current = omega.reshape(-1, CAP, width, width)
    row_lists = block_rows.reshape(-1, CAP)
    col_lists = block_cols.reshape(-1, CAP)
    for iteration in range(ITERS):

        def accumulate(totals, item):
            blocks, row_ids, col_ids = item
            active = row_ids >= 0
            picked = samples[jnp.where(active, col_ids, 0)]
            products = jnp.einsum('snk,sbk->snb', picked, blocks, precision=lax.Precision.HIGHEST)
            target = jnp.where(active, row_ids, total_blocks)
            return (totals.at[target].add(products, mode='drop'), None)
        start_totals = jnp.zeros((total_blocks, sample_count, width), jnp.float32)
        totals, unused = lax.scan(accumulate, start_totals, (current, row_lists, col_lists))

        def update(carry, item):
            blocks, row_ids, col_ids = item
            active = row_ids >= 0
            safe_rows = jnp.where(active, row_ids, 0)
            safe_cols = jnp.where(active, col_ids, 0)
            grad = gradient_blocks(totals[safe_rows], samples[safe_cols], samples[safe_rows], totals[safe_cols], sample_count)
            return (carry, proximal(blocks, grad, active, active & (row_ids == col_ids)))
        unused_carry, current = lax.scan(update, 0, (current, row_lists, col_lists))
    return current.reshape(omega.shape)
```

```python
import functools

import jax
import jax.numpy as jnp
from jax import lax
from jax.experimental import pallas as pl
from jax.experimental.pallas import tpu as pltpu
from jax.sharding import PartitionSpec as P

ITERS = 2
STEP = 0.5
PENALTY = 0.1
VMEM_BYTES = 56 * 1024 * 1024
CORES = 2


def split(x):
    high = x.astype(jnp.bfloat16)
    low = (x - high.astype(jnp.float32)).astype(jnp.bfloat16)
    return high, low


def dot(a, b, dims):
    return lax.dot_general(a, b, (dims, ((), ())), preferred_element_type=jnp.float32)


def product(x, block):
    x_high, x_low = split(x)
    o_high, o_low = split(block)
    count = x.shape[0]
    both = dot(jnp.concatenate([x_high, x_low], 0), o_high, ((1,), (1,)))
    return both[:count] + both[count:] + dot(x_high, o_low, ((1,), (1,)))


def gradient(left_w, right_x, left_x, right_w):
    a_high, a_low = split(jnp.concatenate([left_w, left_x], 0))
    b_high, b_low = split(jnp.concatenate([right_x, right_w], 0))
    dims = ((0,), (0,))
    first = dot(jnp.concatenate([a_high, a_low], 0), jnp.concatenate([b_high, b_high], 0), dims)
    return first + dot(a_high, b_low, dims)


def shrink(v):
    level = STEP * PENALTY
    return v - jnp.clip(v, -level, level)


def lift_diagonal(v, shrunk):
    rows = lax.broadcasted_iota(jnp.int32, v.shape, 0)
    cols = lax.broadcasted_iota(jnp.int32, v.shape, 1)
    eye = rows == cols
    entries = jnp.sum(jnp.where(eye, v, 0.0), axis=0, keepdims=True)
    lifted = 0.5 * (entries + jnp.sqrt(entries * entries + 4.0 * STEP))
    return jnp.where(eye, lifted, shrunk)


def block_count(*sizes):
    for count in (16, 8, 4, 2):
        if all(size % count == 0 for size in sizes):
            return count
    return 1


def diag_products_kernel(x_ref, omega_ref, p_ref):
    for k in range(x_ref.shape[0]):
        p_ref[k] = product(x_ref[k], omega_ref[k])


def diag_update_kernel(scale, last, x_ref, w_ref, omega_ref, out_ref, *p_refs):
    for k in range(x_ref.shape[0]):
        x, w = x_ref[k], w_ref[k]
        v = omega_ref[k] - STEP * (gradient(w, x, x, w) * scale)
        new = lift_diagonal(v, shrink(v))
        out_ref[k] = new
        if not last:
            p_refs[0][k] = product(x, new)


def params():
    return pltpu.CompilerParams(vmem_limit_bytes=VMEM_BYTES)


def cost(slots, dims, passes, extra=0):
    count, width = dims
    return pl.CostEstimate(
        flops=2 * slots * passes * count * width * width,
        bytes_accessed=slots * (2 * width * width + 4 * count * width) * 4 + extra,
        transcendentals=0,
    )


def diag_products(x, omega):
    slab, count, width = x.shape
    size = block_count(slab)
    x_spec = pl.BlockSpec((size, count, width), lambda i: (i, 0, 0))
    o_spec = pl.BlockSpec((size, width, width), lambda i: (i, 0, 0))
    return pl.pallas_call(
        diag_products_kernel,
        grid=(slab // size,),
        in_specs=[x_spec, o_spec],
        out_specs=x_spec,
        out_shape=jax.ShapeDtypeStruct(x.shape, jnp.float32),
        compiler_params=params(),
        cost_estimate=cost(slab, (count, width), 3),
        name="diag_products",
    )(x, omega)


def diag_update(x, w, omega, last):
    slab, count, width = x.shape
    size = block_count(slab)
    x_spec = pl.BlockSpec((size, count, width), lambda i: (i, 0, 0))
    o_spec = pl.BlockSpec((size, width, width), lambda i: (i, 0, 0))
    outs = [jax.ShapeDtypeStruct(omega.shape, jnp.float32)]
    specs = [o_spec]
    if not last:
        outs.append(jax.ShapeDtypeStruct(x.shape, jnp.float32))
        specs.append(x_spec)
    return pl.pallas_call(
        functools.partial(diag_update_kernel, 0.5 / count, last),
        grid=(slab // size,),
        in_specs=[x_spec, x_spec, o_spec],
        out_specs=specs,
        out_shape=outs,
        compiler_params=params(),
        cost_estimate=cost(slab, (count, width), 9),
        name="diag_update",
    )(x, w, omega)


def off_kernel(plan, scalars, *refs):
    update, products, scale, size, slab, n_col, n_row, choices = plan
    steps = pl.num_programs(0)
    step = pl.program_id(0)
    refs = list(refs)
    take = lambda n: [refs.pop(0) for _ in range(n)]
    col_x_parts = take(n_col)
    col_w_parts = take(n_col) if update else []
    row_x_parts = take(n_row) if update else []
    row_w_parts = take(n_row) if update else []
    if update:
        take(1)
    (omega_ref,) = take(1)
    out_refs = take(1) if update else []
    p_refs = take(2) if products else []
    col_x = take(1)[0]
    col_w, row_x, row_w = take(3) if update else (None, None, None)
    acc = take(1)[0] if products else None
    (sems,) = take(1)
    (p_sems,) = take(1) if products else (None,)
    z_index = scalars[3, 0]

    copies = []

    def add(condition, source, target):
        copies.append((condition, pltpu.make_async_copy(source, target, sems.at[len(copies)])))

    def columns(parts, target):
        at = 0
        for part in parts:
            add(None, part, target.at[pl.ds(at, part.shape[0])])
            at += part.shape[0]

    def rows(parts, target):
        for part, (at, wanted) in zip(parts, choices):
            condition = None
            if wanted is not None:
                bound, above = wanted
                condition = z_index < bound if above else z_index >= bound
            add(condition, part, target.at[pl.ds(at, part.shape[0])])

    columns(col_x_parts, col_x)
    if update:
        columns(col_w_parts, col_w)
        rows(row_x_parts, row_x)
        rows(row_w_parts, row_w)

    def each(action):
        for condition, copy in copies:
            if condition is None:
                action(copy)
            else:
                pl.when(condition)(functools.partial(action, copy))

    @pl.when(step == 0)
    def _():
        each(lambda copy: copy.start())
        if products:
            acc[...] = jnp.zeros_like(acc)
        each(lambda copy: copy.wait())

    for k in range(size):
        slot = step * size + k
        target = scalars[0, slot]
        column = scalars[1, slot]
        x = col_x[column]
        block = omega_ref[k]
        if update:
            source = scalars[2, slot]
            grad = gradient(row_w[source], x, row_x[source], col_w[column]) * scale
            block = jnp.where(scalars[4, slot] > 0, shrink(block - STEP * grad), 0.0)
            out_refs[0][k] = block
        if products:
            acc[target] += product(x, block)

    if products:

        @pl.when(step == steps - 1)
        def _():
            half = p_refs[0].shape[0]
            outs = [
                pltpu.make_async_copy(acc.at[pl.ds(side * half, half)], p_refs[side], p_sems.at[side])
                for side in range(2)
            ]
            for copy in outs:
                copy.start()
            for copy in outs:
                copy.wait()


def off_slots(scalars, col_x, omega, slab, half, choices, state=None, products=True):
    update = state is not None
    cap, width = omega.shape[0], omega.shape[1]
    count = col_x[0].shape[1]
    off = cap - slab
    size = block_count(slab, off)
    any_spec = pl.BlockSpec(memory_space=pl.ANY)
    slots = pl.BlockSpec((size, width, width), lambda i, s: (slab // size + i, 0, 0))
    col_blocks = sum(part.shape[0] for part in col_x)
    block = (count, width)
    operands = list(col_x)
    scratch = [pltpu.VMEM((col_blocks,) + block, jnp.float32)]
    copies = len(col_x)
    n_row = 0
    if update:
        col_w, row_x, row_w, buffer = state
        n_row = len(row_x)
        operands += list(col_w) + list(row_x) + list(row_w) + [buffer]
        scratch += [
            pltpu.VMEM((col_blocks,) + block, jnp.float32),
            pltpu.VMEM((2 * half,) + block, jnp.float32),
            pltpu.VMEM((2 * half,) + block, jnp.float32),
        ]
        copies = 2 * len(col_x) + 2 * n_row
    in_specs = [any_spec] * len(operands) + [slots]
    aliases = {len(operands): 0} if update else {}
    outs, out_specs = [], []
    if update:
        outs.append(jax.ShapeDtypeStruct(omega.shape, jnp.float32))
        out_specs.append(slots)
    if products:
        outs += [jax.ShapeDtypeStruct((half,) + block, jnp.float32)] * 2
        out_specs += [any_spec] * 2
        scratch.append(pltpu.VMEM((2 * half + 1,) + block, jnp.float32))
    scratch.append(pltpu.SemaphoreType.DMA((copies,)))
    if products:
        scratch.append(pltpu.SemaphoreType.DMA((2,)))
    plan = (update, products, 0.5 / count, size, slab, len(col_x), n_row, choices)
    return pl.pallas_call(
        functools.partial(off_kernel, plan),
        grid_spec=pltpu.PrefetchScalarGridSpec(
            num_scalar_prefetch=1,
            grid=(off // size,),
            in_specs=in_specs,
            out_specs=out_specs,
            scratch_shapes=scratch,
        ),
        out_shape=outs,
        input_output_aliases=aliases,
        compiler_params=params(),
        cost_estimate=cost(off, block, 3 * (2 * update + products), 2 * half * count * width * 4),
        name="off_update" if update else "off_products",
    )(scalars, *operands, omega)


def gather_columns(v):
    rows = lax.axis_size("row")
    if rows == 4:
        flip = lambda part, bit: lax.ppermute(part, "row", [(i, i ^ bit) for i in range(rows)])
        middle = v.shape[0] // 2
        first, second = flip(v, 1), flip(v, 2)
        return [v, first, second, flip(first[:middle], 2), flip(second[middle:], 1)]
    shift = lambda d: lax.ppermute(v, "row", [((i + d) % rows, i) for i in range(rows)])
    return [v] + [shift(d) for d in range(1, rows)]


def column_place(group, own, rows):
    return group ^ own if rows == 4 else (group - own) % rows


def swap_cores(v):
    return lax.ppermute(v, "col", [(i, i ^ 1) for i in range(lax.axis_size("col"))])


def pass_on(v, up, sources):
    move = CORES if up else -CORES
    return lax.ppermute(v, "col", [(z * CORES + c, z * CORES + c + move) for z in sources for c in range(CORES)])


def gather_rows(v, chips):
    ups, downs = [], []
    up = down = v
    for hop in range(1, chips):
        up = pass_on(up, True, range(hop - 1, chips - 1))
        down = pass_on(down, False, range(1, chips - hop + 1))
        ups.append(up)
        downs.append(down)
    return ups, downs


def row_parts(v, chips, half):
    slab = v.shape[0]
    ups, downs = gather_rows(v, chips)
    parts, choices = [], []
    for side in range(CORES):
        mine = side == 0
        parts.append(v if mine else swap_cores(v))
        choices.append((side * half, None))
        for distance in range(1, chips):
            down, up = downs[distance - 1], ups[distance - 1]
            at = side * half + slab + (distance - 1) * slab
            parts.append(down if mine else swap_cores(down))
            choices.append((at, (chips - distance, True)))
            at = side * half + slab + (chips - distance - 1) * slab
            parts.append(up if mine else swap_cores(up))
            choices.append((at, (distance, False)))
    return parts, tuple(choices)


def scatter_rows(mine, other, slab, chips):
    def part(relative):
        at = slab + (relative - 1) * slab
        return mine[at : at + slab] + other[at : at + slab]

    up = down = None
    for distance in range(chips - 1, 0, -1):
        next_up, next_down = part(distance), part(chips - distance)
        if up is not None:
            next_up, next_down = next_up + up, next_down + down
        up = pass_on(next_up, True, range(0, chips - distance))
        down = pass_on(next_down, False, range(distance, chips))
    return mine[:slab] + other[:slab] + up + down


def shards(samples, omega, block_rows, block_cols):
    n_row, n_col = lax.axis_size("row"), lax.axis_size("col")
    a, b = lax.axis_index("row"), lax.axis_index("col")
    slab = samples.shape[0]
    chips = n_col // CORES
    chip, core = b // CORES, b % CORES
    half = slab * chips
    blocks = omega[0, 0]
    rows = block_rows[0, 0, slab:]
    cols = block_cols[0, 0, slab:]
    live = rows >= 0
    local = rows - a * (slab * n_col)
    owner, inner = local // slab, local % slab
    side = (owner % CORES) ^ core
    relative = (owner // CORES - chip) % chips
    place = jnp.where(live, side * half + relative * slab + inner, 0)
    target = jnp.where(live, place, CORES * half)
    group = column_place(cols // slab // n_col, a, n_row)
    column = jnp.where(live, group * slab + cols % slab, 0)
    scalars = jnp.stack(
        [target, column, place, jnp.full_like(place, chip), live.astype(jnp.int32)]
    ).astype(jnp.int32)

    col_x = gather_columns(samples)
    row_x, choices = row_parts(samples, chips, half)
    p_diag = diag_products(samples, blocks)
    p_mine, p_other = off_slots(scalars, col_x, blocks, slab, half, choices)
    for iteration in range(ITERS):
        last = iteration == ITERS - 1
        own_w = scatter_rows(p_mine, swap_cores(p_other), slab, chips) + p_diag
        col_w = gather_columns(own_w)
        row_w, _ = row_parts(own_w, chips, half)
        if last:
            (buffer,) = diag_update(samples, own_w, blocks, last)
        else:
            buffer, p_diag = diag_update(samples, own_w, blocks, last)
        result = off_slots(
            scalars, col_x, blocks, slab, half, choices, (col_w, row_x, row_w, buffer), not last
        )
        if last:
            blocks = result[0]
        else:
            blocks, p_mine, p_other = result
    return blocks[None, None]


def solution(mesh):
    return jax.shard_map(
        shards,
        mesh=mesh,
        in_specs=(
            P(("row", "col"), None, None),
            P("row", "col", None, None, None),
            P("row", "col", None),
            P("row", "col", None),
        ),
        out_specs=P("row", "col", None, None, None),
        check_vma=False,
    )
```

```python
import functools

import jax
import jax.numpy as jnp
from jax import lax
from jax.experimental import pallas as pl
from jax.experimental.pallas import tpu as pltpu
from jax.sharding import PartitionSpec as P

ITERS = 2
STEP = 0.5
PENALTY = 0.1
VMEM_BYTES = 56 * 1024 * 1024
CORES = 2
TIERS = ((21, 18, 15), (23, 20, 17), (26, 23, 20), (1 << 30,))


def split(x):
    high = x.astype(jnp.bfloat16)
    low = (x - high.astype(jnp.float32)).astype(jnp.bfloat16)
    return high, low


def dot(a, b, dims):
    return lax.dot_general(a, b, (dims, ((), ())), preferred_element_type=jnp.float32)


def product(x, block):
    x_high, x_low = split(x)
    o_high, o_low = split(block)
    count = x.shape[0]
    both = dot(jnp.concatenate([x_high, x_low], 0), o_high, ((1,), (1,)))
    return both[:count] + both[count:] + dot(x_high, o_low, ((1,), (1,)))


def gradient(left_w, right_x, left_x, right_w):
    a_high, a_low = split(jnp.concatenate([left_w, left_x], 0))
    b_high, b_low = split(jnp.concatenate([right_x, right_w], 0))
    dims = ((0,), (0,))
    first = dot(jnp.concatenate([a_high, a_low], 0), jnp.concatenate([b_high, b_high], 0), dims)
    return first + dot(a_high, b_low, dims)


def shrink(v):
    level = STEP * PENALTY
    return v - jnp.clip(v, -level, level)


def lift_diagonal(v, shrunk):
    rows = lax.broadcasted_iota(jnp.int32, v.shape, 0)
    cols = lax.broadcasted_iota(jnp.int32, v.shape, 1)
    eye = rows == cols
    entries = jnp.sum(jnp.where(eye, v, 0.0), axis=0, keepdims=True)
    lifted = 0.5 * (entries + jnp.sqrt(entries * entries + 4.0 * STEP))
    return jnp.where(eye, lifted, shrunk)


def block_count(*sizes):
    for count in (16, 8, 4, 2):
        if all(size % count == 0 for size in sizes):
            return count
    return 1


def diag_products_kernel(x_ref, omega_ref, p_ref):
    for k in range(x_ref.shape[0]):
        p_ref[k] = product(x_ref[k], omega_ref[k])


def diag_update_kernel(scale, last, x_ref, w_ref, omega_ref, out_ref, *p_refs):
    for k in range(x_ref.shape[0]):
        x, w = x_ref[k], w_ref[k]
        v = omega_ref[k] - STEP * (gradient(w, x, x, w) * scale)
        new = lift_diagonal(v, shrink(v))
        out_ref[k] = new
        if not last:
            p_refs[0][k] = product(x, new)


def params():
    return pltpu.CompilerParams(vmem_limit_bytes=VMEM_BYTES)


def cost(slots, dims, passes, extra=0):
    count, width = dims
    return pl.CostEstimate(
        flops=2 * slots * passes * count * width * width,
        bytes_accessed=slots * (2 * width * width + 4 * count * width) * 4 + extra,
        transcendentals=0,
    )


def diag_products(x, omega):
    slab, count, width = x.shape
    size = block_count(slab)
    x_spec = pl.BlockSpec((size, count, width), lambda i: (i, 0, 0))
    o_spec = pl.BlockSpec((size, width, width), lambda i: (i, 0, 0))
    return pl.pallas_call(
        diag_products_kernel,
        grid=(slab // size,),
        in_specs=[x_spec, o_spec],
        out_specs=x_spec,
        out_shape=jax.ShapeDtypeStruct(x.shape, jnp.float32),
        compiler_params=params(),
        cost_estimate=cost(slab, (count, width), 3),
        name="diag_products",
    )(x, omega)


def diag_update(x, w, omega, last):
    slab, count, width = x.shape
    size = block_count(slab)
    x_spec = pl.BlockSpec((size, count, width), lambda i: (i, 0, 0))
    o_spec = pl.BlockSpec((size, width, width), lambda i: (i, 0, 0))
    outs = [jax.ShapeDtypeStruct(omega.shape, jnp.float32)]
    specs = [o_spec]
    if not last:
        outs.append(jax.ShapeDtypeStruct(x.shape, jnp.float32))
        specs.append(x_spec)
    return pl.pallas_call(
        functools.partial(diag_update_kernel, 0.5 / count, last),
        grid=(slab // size,),
        in_specs=[x_spec, x_spec, o_spec],
        out_specs=specs,
        out_shape=outs,
        compiler_params=params(),
        cost_estimate=cost(slab, (count, width), 9),
        name="diag_update",
    )(x, w, omega)


def off_kernel(plan, scalars, *refs):
    update, products, scale, size, n_col, x_choices, w_choices = plan
    steps = pl.num_programs(0)
    step = pl.program_id(0)
    refs = list(refs)
    take = lambda n: [refs.pop(0) for _ in range(n)]
    col_x_parts = take(n_col)
    col_w_parts = take(n_col) if update else []
    row_x_parts = take(len(x_choices)) if update else []
    row_w_parts = take(len(w_choices)) if update else []
    if update:
        take(1)
    (omega_ref,) = take(1)
    out_refs = take(1) if update else []
    p_refs = take(2) if products else []
    col_x = take(1)[0]
    col_w, row_x, row_w = take(3) if update else (None, None, None)
    acc = take(1)[0] if products else None
    (sems,) = take(1)
    (p_sems,) = take(1) if products else (None,)
    z_index = scalars[3, 0]

    copies = []

    def add(condition, source, target):
        copies.append((condition, pltpu.make_async_copy(source, target, sems.at[len(copies)])))

    def columns(parts, target):
        at = 0
        for part in parts:
            add(None, part, target.at[pl.ds(at, part.shape[0])])
            at += part.shape[0]

    def rows(parts, choices, target):
        for part, (at, wanted) in zip(parts, choices):
            condition = None
            if wanted is not None:
                bound, above = wanted
                condition = z_index < bound if above else z_index >= bound
            add(condition, part, target.at[pl.ds(at, part.shape[0])])

    columns(col_x_parts, col_x)
    if update:
        columns(col_w_parts, col_w)
        rows(row_x_parts, x_choices, row_x)
        rows(row_w_parts, w_choices, row_w)

    def each(action):
        for condition, copy in copies:
            if condition is None:
                action(copy)
            else:
                pl.when(condition)(functools.partial(action, copy))

    @pl.when(step == 0)
    def _():
        each(lambda copy: copy.start())
        if products:
            acc[...] = jnp.zeros_like(acc)
        each(lambda copy: copy.wait())

    for k in range(size):
        slot = step * size + k
        target = scalars[0, slot]
        column = scalars[1, slot]
        x = col_x[column]
        block = omega_ref[k]
        if update:
            row_at, x_at = scalars[5, slot], scalars[2, slot]
            grad = gradient(row_w[row_at], x, row_x[x_at], col_w[column]) * scale
            block = jnp.where(scalars[4, slot] > 0, shrink(block - STEP * grad), 0.0)
            out_refs[0][k] = block
        if products:
            acc[target] += product(x, block)

    if products:

        @pl.when(step == steps - 1)
        def _():
            half = p_refs[0].shape[0]
            outs = [
                pltpu.make_async_copy(acc.at[pl.ds(side * half, half)], p_refs[side], p_sems.at[side])
                for side in range(2)
            ]
            for copy in outs:
                copy.start()
            for copy in outs:
                copy.wait()


def off_slots(scalars, col_x, omega, slab, half, state=None, products=True):
    update = state is not None
    cap, width = omega.shape[0], omega.shape[1]
    count = col_x[0].shape[1]
    off = cap - slab
    size = block_count(slab, off)
    any_spec = pl.BlockSpec(memory_space=pl.ANY)
    slots = pl.BlockSpec((size, width, width), lambda i, s: (slab // size + i, 0, 0))
    col_blocks = sum(part.shape[0] for part in col_x)
    block = (count, width)
    operands = list(col_x)
    scratch = [pltpu.VMEM((col_blocks,) + block, jnp.float32)]
    copies = len(col_x)
    x_choices = w_choices = ()
    if update:
        col_w, (row_x, x_choices), (row_w, w_choices), buffer = state
        operands += list(col_w) + list(row_x) + list(row_w) + [buffer]
        x_rows = max(at + part.shape[0] for part, (at, _) in zip(row_x, x_choices))
        scratch += [
            pltpu.VMEM((col_blocks,) + block, jnp.float32),
            pltpu.VMEM((x_rows,) + block, jnp.float32),
            pltpu.VMEM((CORES * half,) + block, jnp.float32),
        ]
        copies = 2 * len(col_x) + len(row_x) + len(row_w)
    in_specs = [any_spec] * len(operands) + [slots]
    aliases = {len(operands): 0} if update else {}
    outs, out_specs = [], []
    if update:
        outs.append(jax.ShapeDtypeStruct(omega.shape, jnp.float32))
        out_specs.append(slots)
    if products:
        outs += [jax.ShapeDtypeStruct((half,) + block, jnp.float32)] * 2
        out_specs += [any_spec] * 2
        scratch.append(pltpu.VMEM((CORES * half + 1,) + block, jnp.float32))
    scratch.append(pltpu.SemaphoreType.DMA((copies,)))
    if products:
        scratch.append(pltpu.SemaphoreType.DMA((2,)))
    plan = (update, products, 0.5 / count, size, len(col_x), x_choices, w_choices)
    return pl.pallas_call(
        functools.partial(off_kernel, plan),
        grid_spec=pltpu.PrefetchScalarGridSpec(
            num_scalar_prefetch=1,
            grid=(off // size,),
            in_specs=in_specs,
            out_specs=out_specs,
            scratch_shapes=scratch,
        ),
        out_shape=outs,
        input_output_aliases=aliases,
        compiler_params=params(),
        cost_estimate=cost(off, block, 3 * (2 * update + products), 2 * half * count * width * 4),
        name="off_update" if update else "off_products",
    )(scalars, *operands, omega)


def combine_kernel(places, mine_ref, other_ref, diag_ref, up_ref, down_ref, w_ref, up_out, down_out):
    most = up_ref.shape[0]
    for i in range(w_ref.shape[0]):
        up_place, down_place = places[0, i], places[1, i]
        w = mine_ref[i] + other_ref[i] + diag_ref[i]
        came_up = jnp.where(down_place < most, up_ref[jnp.minimum(down_place, most - 1)], 0.0)
        came_down = jnp.where(up_place < most, down_ref[jnp.minimum(up_place, most - 1)], 0.0)
        w = w + (came_up + came_down)
        w_ref[i] = w

        @pl.when(up_place < most)
        def _():
            up_out[up_place] = w

        @pl.when(down_place < most)
        def _():
            down_out[down_place] = w


def combine(places, mine, other, diag, up, down):
    slab, most, block = diag.shape[0], up.shape[0], diag.shape[1:]
    whole = lambda n: pl.BlockSpec((n,) + block, lambda i, s: (0, 0, 0))
    shape = lambda n: jax.ShapeDtypeStruct((n,) + block, jnp.float32)
    return pl.pallas_call(
        combine_kernel,
        grid_spec=pltpu.PrefetchScalarGridSpec(
            num_scalar_prefetch=1,
            grid=(1,),
            in_specs=[whole(slab)] * 3 + [whole(most)] * 2,
            out_specs=[whole(slab), whole(most), whole(most)],
        ),
        out_shape=[shape(slab), shape(most), shape(most)],
        compiler_params=params(),
        name="combine",
    )(places, mine, other, diag, up, down)


def together(*values):
    return lax.optimization_barrier(values)


def flip_row(part, bit):
    return lax.ppermute(part, "row", [(i, i ^ bit) for i in range(lax.axis_size("row"))])


def columns_first(v):
    rows = lax.axis_size("row")
    if rows == 4:
        return [flip_row(v, 1), flip_row(v, 2)]
    return [lax.ppermute(v, "row", [((i + d) % rows, i) for i in range(rows)]) for d in range(1, rows)]


def columns_second(first):
    if lax.axis_size("row") != 4:
        return []
    middle = first[0].shape[0] // 2
    return [flip_row(first[0][:middle], 2), flip_row(first[1][middle:], 1)]


def column_place(group, own, rows):
    return group ^ own if rows == 4 else (group - own) % rows


def swap_cores(v):
    return lax.ppermute(v, "col", [(i, i ^ 1) for i in range(lax.axis_size("col"))])


def pass_on(v, up, sources):
    move = CORES if up else -CORES
    return lax.ppermute(v, "col", [(z * CORES + c, z * CORES + c + move) for z in sources for c in range(CORES)])


def hop_both(up, down, hop, chips):
    return (
        pass_on(up, True, range(hop - 1, chips - 1)),
        pass_on(down, False, range(1, chips - hop + 1)),
    )


def row_parts(own, ups, downs, most):
    slab, chips = own[0].shape[0], len(ups) + 1
    half = slab + (chips - 1) * most
    parts, choices = [], []
    for side in range(CORES):
        parts.append(own[side])
        choices.append((side * half, None))
        for distance in range(1, chips):
            start = side * half + slab
            parts.append(downs[distance - 1][side])
            choices.append((start + (distance - 1) * most, (chips - distance, True)))
            parts.append(ups[distance - 1][side])
            choices.append((start + (chips - distance - 1) * most, (distance, False)))
    return parts, tuple(choices)


def scatter_rows(mine, other, slab, chips, limits):
    most = limits[0]

    def part(relative, size):
        at = slab + (relative - 1) * most
        return mine[at : at + size] + other[at : at + size]

    up = down = None
    for distance in range(chips - 1, 0, -1):
        size = limits[distance - 1]
        next_up, next_down = part(distance, size), part(chips - distance, size)
        if up is not None:
            next_up, next_down = next_up.at[: up.shape[0]].add(up), next_down.at[: down.shape[0]].add(down)
        up, down = together(
            pass_on(next_up, True, range(0, chips - distance)),
            pass_on(next_down, False, range(distance, chips)),
        )
    return up, down


def ranks(reach, slab):
    inner = jnp.arange(slab)
    key = reach.reshape(-1, slab) * slab + (slab - 1 - inner)
    ahead = key[:, None, :] > key[:, :, None]
    return jnp.sum(ahead.astype(jnp.int32), axis=2).reshape(-1)


def line_pattern(local, live, slab, chips, chip):
    group_rows = slab * chips * CORES
    wanted = jnp.any((local[:, None] == jnp.arange(group_rows)[None, :]) & live[:, None], axis=0)
    wanted = wanted.astype(jnp.int32)
    wanted = jnp.maximum(wanted, swap_cores(wanted))
    ring = lambda d: lax.ppermute(
        wanted,
        "col",
        [((z + d) % chips * CORES + c, z * CORES + c) for z in range(chips) for c in range(CORES)],
    )
    by_relative = jnp.stack([wanted] + [ring(d) for d in range(1, chips)])
    wanters = (chip + jnp.arange(chips)) % chips
    owners = jnp.arange(group_rows) // (slab * CORES)
    away = (wanters[:, None] - owners[None, :]) * by_relative
    return jnp.maximum(jnp.max(away, axis=0), 0), jnp.maximum(-jnp.min(away, axis=0), 0)


def list_sizes(up_reach, down_reach, slab, chips):
    hops = jnp.arange(1, chips)[:, None, None]
    count = lambda reach: jnp.max(jnp.sum((reach.reshape(1, -1, slab) >= hops).astype(jnp.int32), axis=2), axis=1)
    sizes = jnp.maximum(count(up_reach), count(down_reach))
    rows = lax.axis_size("row")
    others = [lax.ppermute(sizes, "row", [((i + d) % rows, i) for i in range(rows)]) for d in range(1, rows)]
    return functools.reduce(jnp.maximum, others, sizes)


def iterate(limits, slab, chips, scalars, places, samples, blocks, p_diag, col_x, x_own, x_ups, x_downs):
    most = limits[0]
    half = slab + (chips - 1) * most
    p_mine, p_other = off_slots(scalars, col_x, blocks, slab, half)
    row_x = None
    for iteration in range(ITERS):
        last = iteration == ITERS - 1
        other = swap_cores(p_other)
        up, down = scatter_rows(p_mine, other, slab, chips, limits)
        own_w, up, down = combine(places, p_mine, other, p_diag, up, down)
        if row_x is None:
            x_up, x_down = hop_both(x_ups[-1][0], x_downs[-1][0], len(x_ups) + 1, chips)
            x_ups = x_ups + [(x_up, swap_cores(x_up))]
            x_downs = x_downs + [(x_down, swap_cores(x_down))]
            row_x = row_parts(x_own, x_ups, x_downs, slab)
        first = columns_first(own_w)
        w_own = (own_w, swap_cores(own_w))
        updated = diag_update(samples, own_w, blocks, last)
        w_ups, w_downs = [], []
        for hop in range(1, chips):
            size = limits[hop - 1]
            up, down = hop_both(up[:size], down[:size], hop, chips)
            if hop == chips - 2:
                up, down, first, w_own, updated, w_ups, w_downs = together(
                    up, down, first, w_own, updated, w_ups, w_downs
                )
            else:
                up, down = together(up, down)
            w_ups.append((up, swap_cores(up)))
            w_downs.append((down, swap_cores(down)))
        col_w = [own_w] + first + columns_second(first)
        row_w = row_parts(w_own, w_ups, w_downs, most)
        result = off_slots(scalars, col_x, blocks, slab, half, (col_w, row_x, row_w, updated[0]), not last)
        blocks = result[0]
        if not last:
            p_diag, (p_mine, p_other) = updated[1], result[1:]
    return blocks


def shards(samples, omega, block_rows, block_cols):
    n_row, n_col = lax.axis_size("row"), lax.axis_size("col")
    a, b = lax.axis_index("row"), lax.axis_index("col")
    slab = samples.shape[0]
    chips = n_col // CORES
    chip, core = b // CORES, b % CORES
    blocks = omega[0, 0]
    rows = block_rows[0, 0, slab:]
    cols = block_cols[0, 0, slab:]

    first = columns_first(samples)
    x_own = (samples, swap_cores(samples))
    x_ups, x_downs = [], []
    up = down = samples
    for hop in range(1, chips - 1):
        up, down = hop_both(up, down, hop, chips)
        x_ups.append((up, swap_cores(up)))
        x_downs.append((down, swap_cores(down)))
    col_x = [samples] + first + columns_second(first)
    p_diag = diag_products(samples, blocks)

    live = rows >= 0
    local = rows - a * (slab * n_col)
    up_reach, down_reach = line_pattern(local, live, slab, chips, chip)
    up_rank, down_rank = ranks(up_reach, slab), ranks(down_reach, slab)
    owner, inner = local // slab, local % slab
    side = (owner % CORES) ^ core
    relative = (owner // CORES - chip) % chips
    pick = lambda table: jnp.sum(
        jnp.where(local[:, None] == jnp.arange(table.shape[0])[None, :], table[None, :], 0), axis=1
    )
    listed = jnp.where(owner // CORES > chip, pick(down_rank), pick(up_rank))
    group = column_place(cols // slab // n_col, a, n_row)
    column = jnp.where(live, group * slab + cols % slab, 0)
    x_place = jnp.where(live, (side * chips + relative) * slab + inner, 0)
    own_ranks = lambda table: lax.dynamic_slice_in_dim(table, b * slab, slab)
    places = jnp.stack([own_ranks(up_rank), own_ranks(down_rank)]).astype(jnp.int32)

    def branch(limits):
        half = slab + (chips - 1) * limits[0]

        def run(samples, blocks, p_diag, col_x, x_own, x_ups, x_downs):
            inside = jnp.where(relative == 0, inner, slab + (relative - 1) * limits[0] + listed)
            place = jnp.where(live, side * half + inside, 0)
            target = jnp.where(live, place, CORES * half)
            scalars = jnp.stack(
                [target, column, x_place, jnp.full_like(place, chip), live.astype(jnp.int32), place]
            ).astype(jnp.int32)
            return iterate(limits, slab, chips, scalars, places, samples, blocks, p_diag, col_x, x_own, x_ups, x_downs)

        return run

    tiers = []
    for tier in TIERS:
        limits = tuple(min(slab, tier[min(hop, len(tier) - 1)]) for hop in range(chips - 1))
        if limits not in tiers:
            tiers.append(limits)
    state = (samples, blocks, p_diag, col_x, x_own, x_ups, x_downs)
    if len(tiers) == 1:
        result = branch(tiers[0])(*state)
    else:
        sizes = list_sizes(up_reach, down_reach, slab, chips)
        too_long = [jnp.any(sizes > jnp.array(limits)).astype(jnp.int32) for limits in tiers[:-1]]
        result = lax.switch(sum(too_long), [branch(limits) for limits in tiers], *state)
    return result[None, None]


def solution(mesh):
    return jax.shard_map(
        shards,
        mesh=mesh,
        in_specs=(
            P(("row", "col"), None, None),
            P("row", "col", None, None, None),
            P("row", "col", None),
            P("row", "col", None),
        ),
        out_specs=P("row", "col", None, None, None),
        check_vma=False,
    )
```

```python
import functools

import jax
import jax.numpy as jnp
from jax import lax
from jax.experimental import pallas as pl
from jax.experimental.pallas import tpu as pltpu
from jax.sharding import PartitionSpec as P

ITERS = 2
STEP = 0.5
PENALTY = 0.1
VMEM_BYTES = 56 * 1024 * 1024
CORES = 2
UNROLL = 4
TIERS = ((21, 18, 15), (23, 20, 17), (26, 23, 20), (1 << 30,))


def split(x):
    high = x.astype(jnp.bfloat16)
    low = (x - high.astype(jnp.float32)).astype(jnp.bfloat16)
    return high, low


def dot(a, b, dims):
    return lax.dot_general(a, b, (dims, ((), ())), preferred_element_type=jnp.float32)


def product(x, block):
    x_high, x_low = split(x)
    o_high, o_low = split(block)
    count = x.shape[0]
    both = dot(jnp.concatenate([x_high, x_low], 0), o_high, ((1,), (1,)))
    return both[:count] + both[count:] + dot(x_high, o_low, ((1,), (1,)))


def gradient(left_w, right_x, left_x, right_w):
    a_high, a_low = split(jnp.concatenate([left_w, left_x], 0))
    b_high, b_low = split(jnp.concatenate([right_x, right_w], 0))
    dims = ((0,), (0,))
    first = dot(jnp.concatenate([a_high, a_low], 0), jnp.concatenate([b_high, b_high], 0), dims)
    return first + dot(a_high, b_low, dims)


def shrink(v):
    level = STEP * PENALTY
    return v - jnp.clip(v, -level, level)


def lift_diagonal(v, shrunk):
    rows = lax.broadcasted_iota(jnp.int32, v.shape, 0)
    cols = lax.broadcasted_iota(jnp.int32, v.shape, 1)
    eye = rows == cols
    entries = jnp.sum(jnp.where(eye, v, 0.0), axis=0, keepdims=True)
    lifted = 0.5 * (entries + jnp.sqrt(entries * entries + 4.0 * STEP))
    return jnp.where(eye, lifted, shrunk)


def block_count(*sizes):
    for count in (16, 8, 4, 2):
        if all(size % count == 0 for size in sizes):
            return count
    return 1


def diag_products_kernel(x_ref, omega_ref, p_ref):
    for k in range(x_ref.shape[0]):
        p_ref[k] = product(x_ref[k], omega_ref[k])


def diag_update_kernel(scale, last, x_ref, w_ref, omega_ref, out_ref, *p_refs):
    for k in range(x_ref.shape[0]):
        x, w = x_ref[k], w_ref[k]
        v = omega_ref[k] - STEP * (gradient(w, x, x, w) * scale)
        new = lift_diagonal(v, shrink(v))
        out_ref[k] = new
        if not last:
            p_refs[0][k] = product(x, new)


def params():
    return pltpu.CompilerParams(vmem_limit_bytes=VMEM_BYTES)


def cost(slots, dims, passes, extra=0):
    count, width = dims
    return pl.CostEstimate(
        flops=2 * slots * passes * count * width * width,
        bytes_accessed=slots * (2 * width * width + 4 * count * width) * 4 + extra,
        transcendentals=0,
    )


def diag_products(x, omega):
    slab, count, width = x.shape
    size = block_count(slab)
    x_spec = pl.BlockSpec((size, count, width), lambda i: (i, 0, 0))
    o_spec = pl.BlockSpec((size, width, width), lambda i: (i, 0, 0))
    return pl.pallas_call(
        diag_products_kernel,
        grid=(slab // size,),
        in_specs=[x_spec, o_spec],
        out_specs=x_spec,
        out_shape=jax.ShapeDtypeStruct(x.shape, jnp.float32),
        compiler_params=params(),
        cost_estimate=cost(slab, (count, width), 3),
        name="diag_products",
    )(x, omega)


def diag_update(x, w, omega, last):
    slab, count, width = x.shape
    size = block_count(slab)
    x_spec = pl.BlockSpec((size, count, width), lambda i: (i, 0, 0))
    o_spec = pl.BlockSpec((size, width, width), lambda i: (i, 0, 0))
    outs = [jax.ShapeDtypeStruct(omega.shape, jnp.float32)]
    specs = [o_spec]
    if not last:
        outs.append(jax.ShapeDtypeStruct(x.shape, jnp.float32))
        specs.append(x_spec)
    return pl.pallas_call(
        functools.partial(diag_update_kernel, 0.5 / count, last),
        grid=(slab // size,),
        in_specs=[x_spec, x_spec, o_spec],
        out_specs=specs,
        out_shape=outs,
        compiler_params=params(),
        cost_estimate=cost(slab, (count, width), 9),
        name="diag_update",
    )(x, w, omega)


def off_kernel(plan, scalars, *refs):
    update, products, scale, size, unroll, n_col, choices = plan
    steps = pl.num_programs(0)
    step = pl.program_id(0)
    refs = list(refs)
    take = lambda n: [refs.pop(0) for _ in range(n)]
    col_x_parts = take(n_col)
    col_w_parts = take(n_col) if update else []
    row_x_parts = take(len(choices)) if update else []
    row_w_parts = take(len(choices)) if update else []
    if update:
        take(1)
    (omega_ref,) = take(1)
    out_refs = take(1) if update else []
    p_refs = take(2) if products else []
    col_x = take(1)[0]
    col_w, row_x, row_w = take(3) if update else (None, None, None)
    acc = take(1)[0] if products else None
    (sems,) = take(1)
    (p_sems,) = take(1) if products else (None,)
    z_index = scalars[3, 0]

    copies = []

    def add(condition, source, target):
        copies.append((condition, pltpu.make_async_copy(source, target, sems.at[len(copies)])))

    def columns(parts, target):
        at = 0
        for part in parts:
            add(None, part, target.at[pl.ds(at, part.shape[0])])
            at += part.shape[0]

    def rows(parts, target):
        for part, (at, wanted) in zip(parts, choices):
            condition = None
            if wanted is not None:
                bound, above = wanted
                condition = z_index < bound if above else z_index >= bound
            add(condition, part, target.at[pl.ds(at, part.shape[0])])

    columns(col_x_parts, col_x)
    if update:
        columns(col_w_parts, col_w)
        rows(row_x_parts, row_x)
        rows(row_w_parts, row_w)

    def each(action):
        for condition, copy in copies:
            if condition is None:
                action(copy)
            else:
                pl.when(condition)(functools.partial(action, copy))

    @pl.when(step == 0)
    def _():
        each(lambda copy: copy.start())
        if products:
            acc[...] = jnp.zeros_like(acc)
        each(lambda copy: copy.wait())

    def one_slot(k):
        slot = step * size + k
        target = scalars[0, slot]
        column = scalars[1, slot]
        x = col_x[column]
        block = omega_ref[k]
        if update:
            row = scalars[2, slot]
            grad = gradient(row_w[row], x, row_x[row], col_w[column]) * scale
            block = jnp.where(scalars[4, slot] > 0, shrink(block - STEP * grad), 0.0)
            out_refs[0][k] = block
        if products:
            acc[target] += product(x, block)

    def some_slots(i, carry):
        for j in range(unroll):
            one_slot(i * unroll + j)
        return carry

    lax.fori_loop(0, size // unroll, some_slots, 0)

    if products:

        @pl.when(step == steps - 1)
        def _():
            half = p_refs[0].shape[0]
            outs = [
                pltpu.make_async_copy(acc.at[pl.ds(side * half, half)], p_refs[side], p_sems.at[side])
                for side in range(2)
            ]
            for copy in outs:
                copy.start()
            for copy in outs:
                copy.wait()


def off_slots(scalars, col_x, omega, slab, half, state=None, products=True):
    update = state is not None
    cap, width = omega.shape[0], omega.shape[1]
    count = col_x[0].shape[1]
    off = cap - slab
    size = block_count(slab, off)
    any_spec = pl.BlockSpec(memory_space=pl.ANY)
    slots = pl.BlockSpec((size, width, width), lambda i, s: (slab // size + i, 0, 0))
    col_blocks = sum(part.shape[0] for part in col_x)
    block = (count, width)
    operands = list(col_x)
    scratch = [pltpu.VMEM((col_blocks,) + block, jnp.float32)]
    copies = len(col_x)
    choices = ()
    if update:
        col_w, row_x, row_w, choices, buffer = state
        operands += list(col_w) + list(row_x) + list(row_w) + [buffer]
        scratch += [
            pltpu.VMEM((col_blocks,) + block, jnp.float32),
            pltpu.VMEM((CORES * half,) + block, jnp.float32),
            pltpu.VMEM((CORES * half,) + block, jnp.float32),
        ]
        copies = 2 * len(col_x) + len(row_x) + len(row_w)
    in_specs = [any_spec] * len(operands) + [slots]
    aliases = {len(operands): 0} if update else {}
    outs, out_specs = [], []
    if update:
        outs.append(jax.ShapeDtypeStruct(omega.shape, jnp.float32))
        out_specs.append(slots)
    if products:
        outs += [jax.ShapeDtypeStruct((half,) + block, jnp.float32)] * 2
        out_specs += [any_spec] * 2
        scratch.append(pltpu.VMEM((CORES * half + 1,) + block, jnp.float32))
    scratch.append(pltpu.SemaphoreType.DMA((copies,)))
    if products:
        scratch.append(pltpu.SemaphoreType.DMA((2,)))
    unroll = UNROLL if size % UNROLL == 0 else 1
    plan = (update, products, 0.5 / count, size, unroll, len(col_x), choices)
    return pl.pallas_call(
        functools.partial(off_kernel, plan),
        grid_spec=pltpu.PrefetchScalarGridSpec(
            num_scalar_prefetch=1,
            grid=(off // size,),
            in_specs=in_specs,
            out_specs=out_specs,
            scratch_shapes=scratch,
        ),
        out_shape=outs,
        input_output_aliases=aliases,
        compiler_params=params(),
        cost_estimate=cost(off, block, 3 * (2 * update + products), 2 * half * count * width * 4),
        name="off_update" if update else "off_products",
    )(scalars, *operands, omega)


def combine_kernel(places, mine_ref, other_ref, diag_ref, up_ref, down_ref, w_ref, up_out, down_out):
    most = up_ref.shape[0]
    for i in range(w_ref.shape[0]):
        up_place, down_place = places[0, i], places[1, i]
        w = mine_ref[i] + other_ref[i] + diag_ref[i]
        came_up = jnp.where(down_place < most, up_ref[jnp.minimum(down_place, most - 1)], 0.0)
        came_down = jnp.where(up_place < most, down_ref[jnp.minimum(up_place, most - 1)], 0.0)
        w = w + (came_up + came_down)
        w_ref[i] = w

        @pl.when(up_place < most)
        def _():
            up_out[up_place] = w

        @pl.when(down_place < most)
        def _():
            down_out[down_place] = w


def combine(places, mine, other, diag, up, down):
    slab, most, block = diag.shape[0], up.shape[0], diag.shape[1:]
    whole = lambda n: pl.BlockSpec((n,) + block, lambda i, s: (0, 0, 0))
    shape = lambda n: jax.ShapeDtypeStruct((n,) + block, jnp.float32)
    return pl.pallas_call(
        combine_kernel,
        grid_spec=pltpu.PrefetchScalarGridSpec(
            num_scalar_prefetch=1,
            grid=(1,),
            in_specs=[whole(slab)] * 3 + [whole(most)] * 2,
            out_specs=[whole(slab), whole(most), whole(most)],
        ),
        out_shape=[shape(slab), shape(most), shape(most)],
        compiler_params=params(),
        name="combine",
    )(places, mine, other, diag, up, down)


def pack_kernel(places, x_ref, up_out, down_out):
    for i in range(x_ref.shape[0]):
        up_out[places[0, i]] = x_ref[i]
        down_out[places[1, i]] = x_ref[i]


def pack(places, x):
    spec = pl.BlockSpec(x.shape, lambda i, s: (0, 0, 0))
    return pl.pallas_call(
        pack_kernel,
        grid_spec=pltpu.PrefetchScalarGridSpec(
            num_scalar_prefetch=1, grid=(1,), in_specs=[spec], out_specs=[spec, spec]
        ),
        out_shape=[jax.ShapeDtypeStruct(x.shape, jnp.float32)] * 2,
        compiler_params=params(),
        name="pack",
    )(places, x)


def together(*values):
    return lax.optimization_barrier(values)


def flip_row(part, bit):
    return lax.ppermute(part, "row", [(i, i ^ bit) for i in range(lax.axis_size("row"))])


def columns_first(v):
    rows = lax.axis_size("row")
    if rows == 4:
        return [flip_row(v, 1), flip_row(v, 2)]
    return [lax.ppermute(v, "row", [((i + d) % rows, i) for i in range(rows)]) for d in range(1, rows)]


def columns_second(first):
    if lax.axis_size("row") != 4:
        return []
    middle = first[0].shape[0] // 2
    return [flip_row(first[0][:middle], 2), flip_row(first[1][middle:], 1)]


def column_place(group, own, rows):
    return group ^ own if rows == 4 else (group - own) % rows


def swap_cores(v):
    return lax.ppermute(v, "col", [(i, i ^ 1) for i in range(lax.axis_size("col"))])


def pass_on(v, up, sources):
    move = CORES if up else -CORES
    return lax.ppermute(v, "col", [(z * CORES + c, z * CORES + c + move) for z in sources for c in range(CORES)])


def hop_both(up, down, hop, chips):
    return (
        pass_on(up, True, range(hop - 1, chips - 1)),
        pass_on(down, False, range(1, chips - hop + 1)),
    )


def row_parts(own, ups, downs, most):
    slab, chips = own[0].shape[0], len(ups) + 1
    half = slab + (chips - 1) * most
    parts, choices = [], []
    for side in range(CORES):
        parts.append(own[side])
        choices.append((side * half, None))
        for distance in range(1, chips):
            start = side * half + slab
            parts.append(downs[distance - 1][side])
            choices.append((start + (distance - 1) * most, (chips - distance, True)))
            parts.append(ups[distance - 1][side])
            choices.append((start + (chips - distance - 1) * most, (distance, False)))
    return parts, tuple(choices)


def scatter_rows(mine, other, slab, chips, limits, beside):
    most = limits[0]

    def part(relative, size):
        at = slab + (relative - 1) * most
        return mine[at : at + size] + other[at : at + size]

    up = down = None
    for distance in range(chips - 1, 0, -1):
        size = limits[distance - 1]
        next_up, next_down = part(distance, size), part(chips - distance, size)
        if up is not None:
            next_up, next_down = next_up.at[: up.shape[0]].add(up), next_down.at[: down.shape[0]].add(down)
        up, down = beside(
            chips - distance,
            (
                pass_on(next_up, True, range(0, chips - distance)),
                pass_on(next_down, False, range(distance, chips)),
            ),
        )
    return up, down


def ranks(reach, slab):
    inner = jnp.arange(slab)
    key = reach.reshape(-1, slab) * slab + (slab - 1 - inner)
    ahead = key[:, None, :] > key[:, :, None]
    return jnp.sum(ahead.astype(jnp.int32), axis=2).reshape(-1)


def line_pattern(local, live, slab, chips, chip):
    group_rows = slab * chips * CORES
    wanted = jnp.any((local[:, None] == jnp.arange(group_rows)[None, :]) & live[:, None], axis=0)
    wanted = wanted.astype(jnp.int32)
    wanted = jnp.maximum(wanted, swap_cores(wanted))
    ring = lambda d: lax.ppermute(
        wanted,
        "col",
        [((z + d) % chips * CORES + c, z * CORES + c) for z in range(chips) for c in range(CORES)],
    )
    by_relative = jnp.stack([wanted] + [ring(d) for d in range(1, chips)])
    wanters = (chip + jnp.arange(chips)) % chips
    owners = jnp.arange(group_rows) // (slab * CORES)
    away = (wanters[:, None] - owners[None, :]) * by_relative
    return jnp.maximum(jnp.max(away, axis=0), 0), jnp.maximum(-jnp.min(away, axis=0), 0)


def list_sizes(up_reach, down_reach, slab, chips):
    hops = jnp.arange(1, chips)[:, None, None]
    count = lambda reach: jnp.max(jnp.sum((reach.reshape(1, -1, slab) >= hops).astype(jnp.int32), axis=2), axis=1)
    sizes = jnp.maximum(count(up_reach), count(down_reach))
    rows = lax.axis_size("row")
    others = [lax.ppermute(sizes, "row", [((i + d) % rows, i) for i in range(rows)]) for d in range(1, rows)]
    return functools.reduce(jnp.maximum, together(*others), sizes)


def iterate(limits, slab, chips, scalars, places, samples, blocks, p_diag, col_x, x_own, x_up, x_down):
    most = limits[0]
    half = slab + (chips - 1) * most
    x_ups, x_downs = [], []
    x_flow = [x_up, x_down]

    def x_hop():
        hop = len(x_ups) + 1
        size = limits[hop - 1]
        x_flow[:] = hop_both(x_flow[0][:size], x_flow[1][:size], hop, chips)
        return x_flow

    def x_arrived(flow):
        x_flow[:] = flow
        x_ups.append((x_flow[0], swap_cores(x_flow[0])))
        x_downs.append((x_flow[1], swap_cores(x_flow[1])))

    first_hop = x_hop()
    p_mine, p_other = off_slots(scalars, col_x, blocks, slab, half)
    row_x = None
    for iteration in range(ITERS):
        last = iteration == ITERS - 1
        other = swap_cores(p_other)
        if iteration == 0:
            other, flow = together(other, tuple(first_hop))
            x_arrived(flow)

        def beside(hop, values):
            if iteration == 0 and len(x_ups) < chips - 1:
                values, flow = together(values, tuple(x_hop()))
                x_arrived(flow)
                return values
            return together(*values)

        up, down = scatter_rows(p_mine, other, slab, chips, limits, beside)
        own_w, up, down = combine(places, p_mine, other, p_diag, up, down)
        first = columns_first(own_w)
        second = []
        w_own = (own_w, swap_cores(own_w))
        updated = diag_update(samples, own_w, blocks, last)
        w_ups, w_downs = [], []
        for hop in range(1, chips):
            size = limits[hop - 1]
            up, down = hop_both(up[:size], down[:size], hop, chips)
            if hop == 1:
                up, down, updated = together(up, down, updated)
            elif hop == chips - 2:
                up, down, first, w_own = together(up, down, first, w_own)
                second = columns_second(first)
            elif hop == chips - 1:
                up, down, second, w_ups, w_downs = together(up, down, second, w_ups, w_downs)
            else:
                up, down = together(up, down)
            w_ups = w_ups + [(up, swap_cores(up))]
            w_downs = w_downs + [(down, swap_cores(down))]
        col_w = [own_w] + first + second
        if row_x is None:
            row_x, choices = row_parts(x_own, x_ups, x_downs, most)
        row_w, _ = row_parts(w_own, w_ups, w_downs, most)
        result = off_slots(scalars, col_x, blocks, slab, half, (col_w, row_x, row_w, choices, updated[0]), not last)
        blocks = result[0]
        if not last:
            p_diag, (p_mine, p_other) = updated[1], result[1:]
    return blocks


def shards(samples, omega, block_rows, block_cols):
    n_row, n_col = lax.axis_size("row"), lax.axis_size("col")
    a, b = lax.axis_index("row"), lax.axis_index("col")
    slab = samples.shape[0]
    chips = n_col // CORES
    chip, core = b // CORES, b % CORES
    blocks = omega[0, 0]
    rows = block_rows[0, 0, slab:]
    cols = block_cols[0, 0, slab:]

    first = columns_first(samples)

    live = rows >= 0
    local = rows - a * (slab * n_col)
    up_reach, down_reach = line_pattern(local, live, slab, chips, chip)
    up_rank, down_rank = ranks(up_reach, slab), ranks(down_reach, slab)
    owner, inner = local // slab, local % slab
    side = (owner % CORES) ^ core
    relative = (owner // CORES - chip) % chips
    pick = lambda table: jnp.sum(
        jnp.where(local[:, None] == jnp.arange(table.shape[0])[None, :], table[None, :], 0), axis=1
    )
    listed = jnp.where(owner // CORES > chip, pick(down_rank), pick(up_rank))
    group = column_place(cols // slab // n_col, a, n_row)
    column = jnp.where(live, group * slab + cols % slab, 0)
    own_ranks = lambda table: lax.dynamic_slice_in_dim(table, b * slab, slab)
    places = jnp.stack([own_ranks(up_rank), own_ranks(down_rank)]).astype(jnp.int32)

    def branch(limits):
        half = slab + (chips - 1) * limits[0]

        def run(*state):
            inside = jnp.where(relative == 0, inner, slab + (relative - 1) * limits[0] + listed)
            place = jnp.where(live, side * half + inside, 0)
            target = jnp.where(live, place, CORES * half)
            scalars = jnp.stack([target, column, place, jnp.full_like(place, chip), live.astype(jnp.int32)])
            return iterate(limits, slab, chips, scalars.astype(jnp.int32), places, *state)

        return run

    tiers = []
    for tier in TIERS:
        limits = tuple(min(slab, tier[min(hop, len(tier) - 1)]) for hop in range(chips - 1))
        if limits not in tiers:
            tiers.append(limits)
    p_diag = diag_products(samples, blocks)
    x_up, x_down = pack(places, samples)
    x_own = (samples, swap_cores(samples))
    if len(tiers) > 1:
        sizes = list_sizes(up_reach, down_reach, slab, chips)
        too_long = [jnp.any(sizes > jnp.array(limits)).astype(jnp.int32) for limits in tiers[:-1]]
        first, tier = together(first, sum(too_long))
    col_x = [samples] + first + columns_second(first)
    state = (samples, blocks, p_diag, col_x, x_own, x_up, x_down)
    if len(tiers) > 1:
        result = lax.switch(tier, [branch(limits) for limits in tiers], *state)
    else:
        result = branch(tiers[0])(*state)
    return result[None, None]


def solution(mesh):
    return jax.shard_map(
        shards,
        mesh=mesh,
        in_specs=(
            P(("row", "col"), None, None),
            P("row", "col", None, None, None),
            P("row", "col", None),
            P("row", "col", None),
        ),
        out_specs=P("row", "col", None, None, None),
        check_vma=False,
    )
```

```python
import functools

import jax
import jax.numpy as jnp
from jax import lax
from jax.experimental import pallas as pl
from jax.experimental.pallas import tpu as pltpu
from jax.sharding import PartitionSpec as P

ITERS = 2
STEP = 0.5
PENALTY = 0.1
VMEM_BYTES = 56 * 1024 * 1024
CORES = 2
UNROLL = 4
TIERS = (15, 17, 19, 1 << 30)
MOST_COLUMNS = 24


def split(x):
    high = x.astype(jnp.bfloat16)
    low = (x - high.astype(jnp.float32)).astype(jnp.bfloat16)
    return high, low


def dot(a, b, dims):
    return lax.dot_general(a, b, (dims, ((), ())), preferred_element_type=jnp.float32)


def product(x, block):
    x_high, x_low = split(x)
    o_high, o_low = split(block)
    count = x.shape[0]
    both = dot(jnp.concatenate([x_high, x_low], 0), o_high, ((1,), (1,)))
    return both[:count] + both[count:] + dot(x_high, o_low, ((1,), (1,)))


def gradient(left_w, right_x, left_x, right_w):
    a_high, a_low = split(jnp.concatenate([left_w, left_x], 0))
    b_high, b_low = split(jnp.concatenate([right_x, right_w], 0))
    dims = ((0,), (0,))
    first = dot(jnp.concatenate([a_high, a_low], 0), jnp.concatenate([b_high, b_high], 0), dims)
    return first + dot(a_high, b_low, dims)


def shrink(v):
    level = STEP * PENALTY
    return v - jnp.clip(v, -level, level)


def lift_diagonal(v, shrunk):
    rows = lax.broadcasted_iota(jnp.int32, v.shape, 0)
    cols = lax.broadcasted_iota(jnp.int32, v.shape, 1)
    eye = rows == cols
    entries = jnp.sum(jnp.where(eye, v, 0.0), axis=0, keepdims=True)
    lifted = 0.5 * (entries + jnp.sqrt(entries * entries + 4.0 * STEP))
    return jnp.where(eye, lifted, shrunk)


def block_count(*sizes):
    for count in (16, 8, 4, 2):
        if all(size % count == 0 for size in sizes):
            return count
    return 1


def each(count, one):
    unroll = UNROLL if count % UNROLL == 0 else 1

    def some(i, carry):
        for j in range(unroll):
            one(i * unroll + j)
        return carry

    lax.fori_loop(0, count // unroll, some, 0)


def diag_products_kernel(x_ref, omega_ref, p_ref):
    def one(k):
        p_ref[k] = product(x_ref[k], omega_ref[k])

    each(x_ref.shape[0], one)


def diag_update_kernel(scale, last, x_ref, w_ref, omega_ref, out_ref, *p_refs):
    def one(k):
        x, w = x_ref[k], w_ref[k]
        v = omega_ref[k] - STEP * (gradient(w, x, x, w) * scale)
        new = lift_diagonal(v, shrink(v))
        out_ref[k] = new
        if not last:
            p_refs[0][k] = product(x, new)

    each(x_ref.shape[0], one)


def params():
    return pltpu.CompilerParams(vmem_limit_bytes=VMEM_BYTES)


def cost(slots, dims, passes, extra=0):
    count, width = dims
    return pl.CostEstimate(
        flops=2 * slots * passes * count * width * width,
        bytes_accessed=slots * (2 * width * width + 4 * count * width) * 4 + extra,
        transcendentals=0,
    )


def diag_products(x, omega):
    slab, count, width = x.shape
    size = block_count(slab)
    x_spec = pl.BlockSpec((size, count, width), lambda i: (i, 0, 0))
    o_spec = pl.BlockSpec((size, width, width), lambda i: (i, 0, 0))
    return pl.pallas_call(
        diag_products_kernel,
        grid=(slab // size,),
        in_specs=[x_spec, o_spec],
        out_specs=x_spec,
        out_shape=jax.ShapeDtypeStruct(x.shape, jnp.float32),
        compiler_params=params(),
        cost_estimate=cost(slab, (count, width), 3),
        name="diag_products",
    )(x, omega)


def diag_update(x, w, omega, last):
    slab, count, width = x.shape
    size = block_count(slab)
    x_spec = pl.BlockSpec((size, count, width), lambda i: (i, 0, 0))
    o_spec = pl.BlockSpec((size, width, width), lambda i: (i, 0, 0))
    outs = [jax.ShapeDtypeStruct(omega.shape, jnp.float32)]
    specs = [o_spec]
    if not last:
        outs.append(jax.ShapeDtypeStruct(x.shape, jnp.float32))
        specs.append(x_spec)
    return pl.pallas_call(
        functools.partial(diag_update_kernel, 0.5 / count, last),
        grid=(slab // size,),
        in_specs=[x_spec, x_spec, o_spec],
        out_specs=specs,
        out_shape=outs,
        compiler_params=params(),
        cost_estimate=cost(slab, (count, width), 9),
        name="diag_update",
    )(x, w, omega)


def off_kernel(plan, scalars, *refs):
    update, products, scale, size, n_col, n_col_w, x_choices, w_choices = plan
    steps = pl.num_programs(0)
    step = pl.program_id(0)
    refs = list(refs)
    take = lambda n: [refs.pop(0) for _ in range(n)]
    col_x_parts = take(n_col)
    col_w_parts = take(n_col_w)
    row_x_parts = take(len(x_choices)) if update else []
    row_w_parts = take(len(w_choices)) if update else []
    if update:
        take(1)
    (omega_ref,) = take(1)
    out_refs = take(1) if update else []
    p_refs = take(2) if products else []
    col_x = take(1)[0]
    col_w, row_x, row_w = take(3) if update else (None, None, None)
    acc = take(1)[0] if products else None
    (sems,) = take(1)
    (p_sems,) = take(1) if products else (None,)
    z_index = scalars[3, 0]

    copies = []

    def add(condition, source, target):
        copies.append((condition, pltpu.make_async_copy(source, target, sems.at[len(copies)])))

    def columns(parts, target):
        at = 0
        for part in parts:
            add(None, part, target.at[pl.ds(at, part.shape[0])])
            at += part.shape[0]

    def rows(parts, choices, target):
        for part, (at, wanted) in zip(parts, choices):
            condition = None
            if wanted is not None:
                bound, above = wanted
                condition = z_index < bound if above else z_index >= bound
            add(condition, part, target.at[pl.ds(at, part.shape[0])])

    columns(col_x_parts, col_x)
    if update:
        columns(col_w_parts, col_w)
        rows(row_x_parts, x_choices, row_x)
        rows(row_w_parts, w_choices, row_w)

    def for_all(action):
        for condition, copy in copies:
            if condition is None:
                action(copy)
            else:
                pl.when(condition)(functools.partial(action, copy))

    @pl.when(step == 0)
    def _():
        for_all(lambda copy: copy.start())
        if products:
            acc[...] = jnp.zeros_like(acc)
        for_all(lambda copy: copy.wait())

    def one_slot(k):
        slot = step * size + k
        target = scalars[0, slot]
        column = scalars[1, slot]
        x = col_x[column]
        block = omega_ref[k]
        if update:
            row_at, x_at = scalars[2, slot], scalars[5, slot]
            grad = gradient(row_w[row_at], x, row_x[x_at], col_w[scalars[6, slot]]) * scale
            block = jnp.where(scalars[4, slot] > 0, shrink(block - STEP * grad), 0.0)
            out_refs[0][k] = block
        if products:
            acc[target] += product(x, block)

    each(size, one_slot)

    if products:

        @pl.when(step == steps - 1)
        def _():
            half = p_refs[0].shape[0]
            outs = [
                pltpu.make_async_copy(acc.at[pl.ds(side * half, half)], p_refs[side], p_sems.at[side])
                for side in range(2)
            ]
            for copy in outs:
                copy.start()
            for copy in outs:
                copy.wait()


def off_slots(scalars, col_x, omega, slab, half, state=None, products=True):
    update = state is not None
    cap, width = omega.shape[0], omega.shape[1]
    count = col_x[0].shape[1]
    off = cap - slab
    size = block_count(slab, off)
    any_spec = pl.BlockSpec(memory_space=pl.ANY)
    slots = pl.BlockSpec((size, width, width), lambda i, s: (slab // size + i, 0, 0))
    col_blocks = sum(part.shape[0] for part in col_x)
    block = (count, width)
    operands = list(col_x)
    scratch = [pltpu.VMEM((col_blocks,) + block, jnp.float32)]
    copies = len(col_x)
    col_w, x_choices, w_choices = (), (), ()
    if update:
        col_w, (row_x, x_choices), (row_w, w_choices), buffer = state
        operands += list(col_w) + list(row_x) + list(row_w) + [buffer]
        row_blocks = lambda parts, choices: max(at + part.shape[0] for part, (at, _) in zip(parts, choices))
        scratch += [
            pltpu.VMEM((sum(part.shape[0] for part in col_w),) + block, jnp.float32),
            pltpu.VMEM((row_blocks(row_x, x_choices),) + block, jnp.float32),
            pltpu.VMEM((row_blocks(row_w, w_choices),) + block, jnp.float32),
        ]
        copies = len(col_x) + len(col_w) + len(row_x) + len(row_w)
    in_specs = [any_spec] * len(operands) + [slots]
    aliases = {len(operands): 0} if update else {}
    outs, out_specs = [], []
    if update:
        outs.append(jax.ShapeDtypeStruct(omega.shape, jnp.float32))
        out_specs.append(slots)
    if products:
        outs += [jax.ShapeDtypeStruct((half,) + block, jnp.float32)] * 2
        out_specs += [any_spec] * 2
        scratch.append(pltpu.VMEM((CORES * half + 1,) + block, jnp.float32))
    scratch.append(pltpu.SemaphoreType.DMA((copies,)))
    if products:
        scratch.append(pltpu.SemaphoreType.DMA((2,)))
    plan = (update, products, 0.5 / count, size, len(col_x), len(col_w), x_choices, w_choices)
    return pl.pallas_call(
        functools.partial(off_kernel, plan),
        grid_spec=pltpu.PrefetchScalarGridSpec(
            num_scalar_prefetch=1,
            grid=(off // size,),
            in_specs=in_specs,
            out_specs=out_specs,
            scratch_shapes=scratch,
        ),
        out_shape=outs,
        input_output_aliases=aliases,
        compiler_params=params(),
        cost_estimate=cost(off, block, 3 * (2 * update + products), 2 * half * count * width * 4),
        name="off_update" if update else "off_products",
    )(scalars, *operands, omega)


def combine_kernel(chips, places, mine_ref, other_ref, diag_ref, *refs):
    came, (w_ref, *sends) = refs[: chips - 1], refs[chips - 1 :]
    most = came[0].shape[0]
    def one(i):
        at = [places[r, i] for r in range(len(sends))]
        w = mine_ref[i] + other_ref[i] + diag_ref[i]
        for r in range(1, chips):
            place = at[chips - r - 1]
            w = w + jnp.where(place < most, came[r - 1][jnp.minimum(place, most - 1)], 0.0)
        w_ref[i] = w
        for place, send in zip(at, sends):

            @pl.when(place < send.shape[0])
            def _(place=place, send=send):
                send[place] = w

    each(w_ref.shape[0], one)


def combine(places, mine, other, diag, came, most_columns):
    slab, most, block = diag.shape[0], came[0].shape[0], diag.shape[1:]
    chips = len(came) + 1
    sizes = [slab] + [most] * (chips - 1) + [most_columns] * (places.shape[0] - chips + 1)
    whole = lambda n: pl.BlockSpec((n,) + block, lambda i, s: (0, 0, 0))
    own, *sends = pl.pallas_call(
        functools.partial(combine_kernel, chips),
        grid_spec=pltpu.PrefetchScalarGridSpec(
            num_scalar_prefetch=1,
            grid=(1,),
            in_specs=[whole(slab)] * 3 + [whole(most)] * (chips - 1),
            out_specs=[whole(n) for n in sizes],
        ),
        out_shape=[jax.ShapeDtypeStruct((n,) + block, jnp.float32) for n in sizes],
        compiler_params=params(),
        name="combine",
    )(places, mine, other, diag, *came)
    return own, sends[: chips - 1], sends[chips - 1 :]


def together(*values):
    return lax.optimization_barrier(values)


def flip_row(part, bit):
    return lax.ppermute(part, "row", [(i, i ^ bit) for i in range(lax.axis_size("row"))])


def from_row(v, d, back=False):
    rows = lax.axis_size("row")
    if rows == 4:
        return flip_row(v, d)
    pairs = [((i + d) % rows, i) for i in range(rows)]
    return lax.ppermute(v, "row", [pair[::-1] for pair in pairs] if back else pairs)


def columns_first(v):
    rows = lax.axis_size("row")
    return [from_row(v, d) for d in range(1, 3 if rows == 4 else rows)]


def columns_second(first):
    if lax.axis_size("row") != 4:
        return []
    middle = first[0].shape[0] // 2
    return [flip_row(first[0][:middle], 2), flip_row(first[1][middle:], 1)]


def column_place(group, own, rows):
    return group ^ own if rows == 4 else (group - own) % rows


def swap_cores(v):
    return lax.ppermute(v, "col", [(i, i ^ 1) for i in range(lax.axis_size("col"))])


def pass_on(v, up, sources):
    move = CORES if up else -CORES
    return lax.ppermute(v, "col", [(z * CORES + c, z * CORES + c + move) for z in sources for c in range(CORES)])


def hop_both(up, down, hop, chips):
    return (
        pass_on(up, True, range(hop - 1, chips - 1)),
        pass_on(down, False, range(1, chips - hop + 1)),
    )


def row_parts(own, ups, downs, most):
    slab, chips = own[0].shape[0], len(ups) + 1
    half = slab + (chips - 1) * most
    parts, choices = [], []
    for side in range(CORES):
        parts.append(own[side])
        choices.append((side * half, None))
        for distance in range(1, chips):
            start = side * half + slab
            parts.append(downs[distance - 1][side])
            choices.append((start + (distance - 1) * most, (chips - distance, True)))
            parts.append(ups[distance - 1][side])
            choices.append((start + (chips - distance - 1) * most, (distance, False)))
    return parts, tuple(choices)


def ring_parts(own, came, most):
    slab, chips = own[0].shape[0], len(came) + 1
    half = slab + (chips - 1) * most
    parts, choices = [], []
    for side in range(CORES):
        parts.append(own[side])
        choices.append((side * half, None))
        for r in range(1, chips):
            parts.append(came[r - 1][side])
            choices.append((side * half + slab + (chips - r - 1) * most, None))
    return parts, tuple(choices)


def round_ring(v, r, chips):
    pairs = [(z * CORES + c, (z + r) % chips * CORES + c) for z in range(chips) for c in range(CORES)]
    return lax.ppermute(v, "col", pairs)


def line_pattern(wanted, chip):
    chips = lax.axis_size("col") // CORES
    wanted = jnp.maximum(wanted, swap_cores(wanted))
    table = jnp.where(jnp.arange(chips)[:, None] == chip, wanted[None], 0)
    steps = chips.bit_length() - 1 if chips & (chips - 1) == 0 else chips - 1
    for step in range(steps):
        there = (lambda z: z ^ 1 << step) if steps < chips - 1 else (lambda z: (z + 1) % chips)
        pairs = [(z * CORES + c, there(z) * CORES + c) for z in range(chips) for c in range(CORES)]
        table = jnp.maximum(table, lax.ppermute(table, "col", pairs))
    return wanted, table


def places_in_lists(wanted, slab):
    before = jnp.arange(slab)[:, None] > jnp.arange(slab)[None, :]
    place = jnp.sum(jnp.where(before, wanted[..., None, :], 0), axis=-1)
    return jnp.where(wanted > 0, place, slab)


def longest_list(table, slab):
    chips = table.shape[0]
    counts = jnp.sum(table.reshape(chips, -1, slab), axis=2)
    own = jnp.arange(chips)[:, None] == jnp.arange(counts.shape[1])[None, :] // CORES
    return jnp.max(jnp.where(own, 0, counts))


def place_of(listed, relative, inner, side, live, slab, chips, most):
    inside = jnp.where(relative == 0, inner, slab + (relative - 1) * most + listed)
    return jnp.where(live, side * (slab + (chips - 1) * most) + inside, 0)


def both_cores(flow):
    return [(part, swap_cores(part)) for part in flow]


def iterate(most, most_columns, stride, slab, chips, scalars, places, samples, blocks, p_diag, col_x, x_own, x_ups, x_downs, p_mine, other):
    half = slab + (chips - 1) * most
    row_x = None
    for iteration in range(ITERS):
        last = iteration == ITERS - 1
        if iteration > 0:
            other = swap_cores(p_other)
        came = []
        for r in range(1, chips):
            at = slab + (r - 1) * stride
            came.append(round_ring(p_mine[at : at + most] + other[at : at + most], r, chips))
        if row_x is None:
            came, flow = together(came, hop_both(x_ups[-1], x_downs[-1], chips - 1, chips))
            x_ups, x_downs = x_ups + [flow[0]], x_downs + [flow[1]]
        own_w, sends, column_sends = combine(places, p_mine, other, p_diag, together(*came), most_columns)
        came = [round_ring(send, r, chips) for r, send in enumerate(sends, 1)]
        w_columns = [from_row(send, d) for d, send in enumerate(column_sends, 1)]
        w_own = (own_w, swap_cores(own_w))
        updated = diag_update(samples, own_w, blocks, last)
        longest = chips // 2 - 1
        rest = came[:longest] + came[longest + 1 :]
        if row_x is None:
            rest, w_columns, updated = together(rest, w_columns, updated)
            row_x = row_parts(x_own, both_cores(x_ups), both_cores(x_downs), slab)
        else:
            rest, w_columns, updated = together(rest, w_columns, updated)
        rest = both_cores(rest)
        came = rest[:longest] + both_cores([came[longest]]) + rest[longest:]
        row_w = ring_parts(w_own, came, most)
        state = ([own_w] + w_columns, row_x, row_w, updated[0])
        result = off_slots(scalars, col_x, blocks, slab, half, state, not last)
        blocks = result[0]
        if not last:
            p_diag, (p_mine, p_other), stride = updated[1], result[1:], most
    return blocks


def shards(samples, omega, block_rows, block_cols):
    n_row, n_col = lax.axis_size("row"), lax.axis_size("col")
    a, b = lax.axis_index("row"), lax.axis_index("col")
    slab = samples.shape[0]
    chips = n_col // CORES
    chip, core = b // CORES, b % CORES
    blocks = omega[0, 0]
    rows = block_rows[0, 0, slab:]
    cols = block_cols[0, 0, slab:]

    first = columns_first(samples)
    x_own = (samples, swap_cores(samples))
    x_ups, x_downs = ([part] for part in hop_both(samples, samples, 1, chips))

    live = rows >= 0
    local = rows - a * (slab * n_col)
    owner, inner = local // slab, local % slab
    side = (owner % CORES) ^ core
    relative = (owner // CORES - chip) % chips
    group, column_inner = column_place(cols // slab // n_col, a, n_row), cols % slab
    column = jnp.where(live, group * slab + column_inner, 0)

    p_diag = diag_products(samples, blocks)
    among = lambda ids, count: jnp.any((ids[:, None] == jnp.arange(count)[None, :]) & live[:, None], axis=0).astype(jnp.int32)
    columns = among(column, n_row * slab).reshape(n_row, slab)
    longest_columns = jnp.max(jnp.sum(columns[1:], axis=1))
    wanted, table = line_pattern(jnp.concatenate([among(local, n_col * slab), longest_columns[None]]), chip)
    x_ups, x_downs, table, first, p_diag = together(x_ups, x_downs, table, first, p_diag)
    for hop in range(2, chips - 1):
        up, down = hop_both(x_ups[-1], x_downs[-1], hop, chips)
        x_ups, x_downs = x_ups + [up], x_downs + [down]
    col_x = [samples] + first + columns_second(first)
    longest_columns = jnp.max(table[:, -1])
    longest = longest_list(table[:, :-1], slab)
    told = [from_row(jnp.concatenate([columns[d], longest[None], longest_columns[None]]), d, True) for d in range(1, n_row)]
    longest, longest_columns = functools.reduce(jnp.maximum, [each[slab:] for each in told], jnp.stack([longest, longest_columns]))
    mine = lax.dynamic_slice_in_dim(table, b * slab, slab, 1)
    ahead = jnp.arange(chips)[None, :] == (chip + jnp.arange(1, chips)[:, None]) % chips
    lists = list(jnp.sum(jnp.where(ahead[:, :, None], mine[None], 0), axis=1)) + [each[:slab] for each in told]
    places = places_in_lists(jnp.stack(lists), slab).astype(jnp.int32)

    pick = lambda table, ids: jnp.sum(jnp.where(ids[:, None] == jnp.arange(table.size)[None, :], table.reshape(1, -1), 0), axis=1)
    listed = pick(places_in_lists(wanted[:-1].reshape(-1, slab), slab), local)
    column_listed = pick(places_in_lists(columns, slab), column)
    place = lambda inner_place, most: place_of(inner_place, relative, inner, side, live, slab, chips, most)
    x_place = place(inner, slab)

    def scalars_of(most, most_columns):
        half = slab + (chips - 1) * most
        at = place(listed, most)
        target = jnp.where(live, at, CORES * half)
        w_column = jnp.where(group == 0, column_inner, slab + (group - 1) * most_columns + column_listed)
        w_column = jnp.where(live, w_column, 0)
        rows = [target, column, at, jnp.full_like(at, chip), live, x_place, w_column]
        return jnp.stack([row.astype(jnp.int32) for row in rows])

    def branch(most):
        most_columns = slab if most == slab else min(slab, MOST_COLUMNS)

        def run(*state):
            scalars = scalars_of(most, most_columns)
            return iterate(most, most_columns, slab, slab, chips, scalars, places, *state)

        return run

    tiers = sorted({min(tier, slab) for tier in TIERS})
    longest = jnp.where(longest_columns > MOST_COLUMNS, slab, longest)
    scalars = scalars_of(slab, slab)
    x_ups, x_downs, col_x, longest, scalars = together(x_ups, x_downs, col_x, longest, scalars)
    p_mine, p_other = off_slots(scalars, col_x, blocks, slab, slab * chips)
    state = (samples, blocks, p_diag, col_x, x_own, x_ups, x_downs, p_mine, swap_cores(p_other))

    def choose(tiers, longest, state):
        if len(tiers) == 1:
            return branch(tiers[0])(*state)
        middle = len(tiers) // 2
        return lax.cond(
            longest <= tiers[middle - 1],
            lambda state: choose(tiers[:middle], longest, state),
            lambda state: choose(tiers[middle:], longest, state),
            state,
        )

    return choose(tiers, longest, state)[None, None]


def solution(mesh):
    return jax.shard_map(
        shards,
        mesh=mesh,
        in_specs=(
            P(("row", "col"), None, None),
            P("row", "col", None, None, None),
            P("row", "col", None),
            P("row", "col", None),
        ),
        out_specs=P("row", "col", None, None, None),
        check_vma=False,
    )
```

```python
import functools
import math

import jax
import jax.numpy as jnp
from jax import lax
from jax.experimental import pallas as pl
from jax.experimental.pallas import tpu as pltpu
from jax.sharding import PartitionSpec as P

ITERS = 2
STEP = 0.5
PENALTY = 0.1
VMEM_SPARE = 20 * 1024 * 1024
CORES = 2
UNROLL = 8
TIERS = (15, 17, 19, 1 << 30)
MOST_COLUMNS = 24


def split(x):
    high = x.astype(jnp.bfloat16)
    low = (x - high.astype(jnp.float32)).astype(jnp.bfloat16)
    return high, low


def dot(a, b, dims):
    return lax.dot_general(a, b, (dims, ((), ())), preferred_element_type=jnp.float32)


def product(x, block):
    x_high, x_low = split(x)
    o_high, o_low = split(block)
    count = x.shape[0]
    dims = ((1,), (1,))
    both = dot(o_high, jnp.concatenate([x_high, x_low], 0), dims)
    return (both[:, :count] + both[:, count:] + dot(o_low, x_high, dims)).T


def gradient(left_w, right_x, left_x, right_w):
    a_high, a_low = split(jnp.concatenate([left_w, left_x], 0))
    b_high, b_low = split(jnp.concatenate([right_x, right_w], 0))
    dims = ((0,), (0,))
    return dot(a_high, b_high, dims) + dot(a_low, b_high, dims) + dot(a_high, b_low, dims)


def shrink(v):
    level = STEP * PENALTY
    return v - jnp.clip(v, -level, level)


def lift_diagonal(v, shrunk):
    rows = lax.broadcasted_iota(jnp.int32, v.shape, 0)
    cols = lax.broadcasted_iota(jnp.int32, v.shape, 1)
    eye = rows == cols
    entries = jnp.sum(jnp.where(eye, v, 0.0), axis=0, keepdims=True)
    lifted = 0.5 * (entries + jnp.sqrt(entries * entries + 4.0 * STEP))
    return jnp.where(eye, lifted, shrunk)


def block_count(*sizes):
    for count in (16, 8, 4, 2):
        if all(size % count == 0 for size in sizes):
            return count
    return 1


def each(count, one):
    unroll = UNROLL if count % UNROLL == 0 else 1

    def some(i, carry):
        for j in range(unroll):
            one(i * unroll + j)
        return carry

    lax.fori_loop(0, count // unroll, some, 0)


def diag_products_kernel(x_ref, omega_ref, p_ref):
    def one(k):
        p_ref[k] = product(x_ref[k], omega_ref[k])

    each(x_ref.shape[0], one)


def diag_update_kernel(scale, last, x_ref, w_ref, omega_ref, out_ref, *p_refs):
    def one(k):
        x, w = x_ref[k], w_ref[k]
        v = omega_ref[k] - STEP * (gradient(w, x, x, w) * scale)
        new = lift_diagonal(v, shrink(v))
        out_ref[k] = new
        if not last:
            p_refs[0][k] = product(x, new)

    each(x_ref.shape[0], one)


def params(*shapes):
    held = sum(4 * math.prod(shape) for shape in shapes)
    return pltpu.CompilerParams(vmem_limit_bytes=held + VMEM_SPARE)


def cost(slots, dims, passes, extra=0):
    count, width = dims
    return pl.CostEstimate(
        flops=2 * slots * passes * count * width * width,
        bytes_accessed=slots * (2 * width * width + 4 * count * width) * 4 + extra,
        transcendentals=0,
    )


def diag_products(x, omega):
    slab, count, width = x.shape
    size = block_count(slab)
    x_spec = pl.BlockSpec((size, count, width), lambda i: (i, 0, 0))
    o_spec = pl.BlockSpec((size, width, width), lambda i: (i, 0, 0))
    return pl.pallas_call(
        diag_products_kernel,
        grid=(slab // size,),
        in_specs=[x_spec, o_spec],
        out_specs=x_spec,
        out_shape=jax.ShapeDtypeStruct(x.shape, jnp.float32),
        compiler_params=params(*[(2 * size, count, width)] * 2, (2 * size, width, width)),
        cost_estimate=cost(slab, (count, width), 3),
        name="diag_products",
    )(x, omega)


def diag_update(x, w, omega, last):
    slab, count, width = x.shape
    size = block_count(slab)
    x_spec = pl.BlockSpec((size, count, width), lambda i: (i, 0, 0))
    o_spec = pl.BlockSpec((size, width, width), lambda i: (i, 0, 0))
    outs = [jax.ShapeDtypeStruct(omega.shape, jnp.float32)]
    specs = [o_spec]
    if not last:
        outs.append(jax.ShapeDtypeStruct(x.shape, jnp.float32))
        specs.append(x_spec)
    return pl.pallas_call(
        functools.partial(diag_update_kernel, 0.5 / count, last),
        grid=(slab // size,),
        in_specs=[x_spec, x_spec, o_spec],
        out_specs=specs,
        out_shape=outs,
        compiler_params=params(*[(2 * size, count, width)] * 3, *[(2 * size, width, width)] * 2),
        cost_estimate=cost(slab, (count, width), 9),
        name="diag_update",
    )(x, w, omega)


def off_kernel(plan, scalars, *refs):
    update, products, scale, size, n_col, n_col_w, x_choices, w_choices = plan
    steps = pl.num_programs(0)
    step = pl.program_id(0)
    refs = list(refs)
    take = lambda n: [refs.pop(0) for _ in range(n)]
    col_x_parts = take(n_col)
    col_w_parts = take(n_col_w)
    row_x_parts = take(len(x_choices)) if update else []
    row_w_parts = take(len(w_choices)) if update else []
    if update:
        take(1)
    (omega_ref,) = take(1)
    out_refs = take(1) if update else []
    p_refs = take(2) if products else []
    col_x = take(1)[0]
    col_w, row_x, row_w = take(3) if update else (None, None, None)
    acc = take(1)[0] if products else None
    (sems,) = take(1)
    (p_sems,) = take(1) if products else (None,)
    z_index = scalars[3, 0]

    copies = []

    def add(condition, source, target):
        copies.append((condition, pltpu.make_async_copy(source, target, sems.at[len(copies)])))

    def columns(parts, target):
        at = 0
        for part in parts:
            add(None, part, target.at[pl.ds(at, part.shape[0])])
            at += part.shape[0]

    def rows(parts, choices, target):
        for part, (at, wanted) in zip(parts, choices):
            condition = None
            if wanted is not None:
                bound, above = wanted
                condition = z_index < bound if above else z_index >= bound
            add(condition, part, target.at[pl.ds(at, part.shape[0])])

    columns(col_x_parts, col_x)
    if update:
        columns(col_w_parts, col_w)
        rows(row_x_parts, x_choices, row_x)
        rows(row_w_parts, w_choices, row_w)

    def for_all(action):
        for condition, copy in copies:
            if condition is None:
                action(copy)
            else:
                pl.when(condition)(functools.partial(action, copy))

    @pl.when(step == 0)
    def _():
        for_all(lambda copy: copy.start())
        if products:
            acc[...] = jnp.zeros_like(acc)
        for_all(lambda copy: copy.wait())

    def one_slot(k):
        slot = step * size + k
        target = scalars[0, slot]
        column = scalars[1, slot]
        x = col_x[column]
        block = omega_ref[k]
        if update:
            row_at, x_at = scalars[2, slot], scalars[5, slot]
            grad = gradient(row_w[row_at], x, row_x[x_at], col_w[scalars[6, slot]]) * scale
            block = jnp.where(scalars[4, slot] > 0, shrink(block - STEP * grad), 0.0)
            out_refs[0][k] = block
        if products:
            acc[target] += product(x, block)

    each(size, one_slot)

    if products:

        @pl.when(step == steps - 1)
        def _():
            half = p_refs[0].shape[0]
            outs = [
                pltpu.make_async_copy(acc.at[pl.ds(side * half, half)], p_refs[side], p_sems.at[side])
                for side in range(2)
            ]
            for copy in outs:
                copy.start()
            for copy in outs:
                copy.wait()


def off_slots(scalars, col_x, omega, slab, half, state=None, products=True):
    update = state is not None
    cap, width = omega.shape[0], omega.shape[1]
    count = col_x[0].shape[1]
    off = cap - slab
    size = block_count(slab, off)
    any_spec = pl.BlockSpec(memory_space=pl.ANY)
    slots = pl.BlockSpec((size, width, width), lambda i, s: (slab // size + i, 0, 0))
    col_blocks = sum(part.shape[0] for part in col_x)
    block = (count, width)
    operands = list(col_x)
    scratch = [pltpu.VMEM((col_blocks,) + block, jnp.float32)]
    copies = len(col_x)
    col_w, x_choices, w_choices = (), (), ()
    if update:
        col_w, (row_x, x_choices), (row_w, w_choices), buffer = state
        operands += list(col_w) + list(row_x) + list(row_w) + [buffer]
        row_blocks = lambda parts, choices: max(at + part.shape[0] for part, (at, _) in zip(parts, choices))
        scratch += [
            pltpu.VMEM((sum(part.shape[0] for part in col_w),) + block, jnp.float32),
            pltpu.VMEM((row_blocks(row_x, x_choices),) + block, jnp.float32),
            pltpu.VMEM((row_blocks(row_w, w_choices),) + block, jnp.float32),
        ]
        copies = len(col_x) + len(col_w) + len(row_x) + len(row_w)
    in_specs = [any_spec] * len(operands) + [slots]
    aliases = {len(operands): 0} if update else {}
    outs, out_specs = [], []
    if update:
        outs.append(jax.ShapeDtypeStruct(omega.shape, jnp.float32))
        out_specs.append(slots)
    if products:
        outs += [jax.ShapeDtypeStruct((half,) + block, jnp.float32)] * 2
        out_specs += [any_spec] * 2
        scratch.append(pltpu.VMEM((CORES * half + 1,) + block, jnp.float32))
    scratch.append(pltpu.SemaphoreType.DMA((copies,)))
    if products:
        scratch.append(pltpu.SemaphoreType.DMA((2,)))
    held = [(4 * size, width, width)] + [each.shape for each in scratch if each.dtype == jnp.float32]
    plan = (update, products, 0.5 / count, size, len(col_x), len(col_w), x_choices, w_choices)
    return pl.pallas_call(
        functools.partial(off_kernel, plan),
        grid_spec=pltpu.PrefetchScalarGridSpec(
            num_scalar_prefetch=1,
            grid=(off // size,),
            in_specs=in_specs,
            out_specs=out_specs,
            scratch_shapes=scratch,
        ),
        out_shape=outs,
        input_output_aliases=aliases,
        compiler_params=params(*held),
        cost_estimate=cost(off, block, 3 * (2 * update + products), 2 * half * count * width * 4),
        name="off_update" if update else "off_products",
    )(scalars, *operands, omega)


def combine_kernel(chips, places, mine_ref, other_ref, diag_ref, *refs):
    came, (w_ref, *sends) = refs[: chips - 1], refs[chips - 1 :]
    most = came[0].shape[0]
    def one(i):
        at = [places[r, i] for r in range(len(sends))]
        w = mine_ref[i] + other_ref[i] + diag_ref[i]
        for r in range(1, chips):
            place = at[chips - r - 1]
            w = w + jnp.where(place < most, came[r - 1][jnp.minimum(place, most - 1)], 0.0)
        w_ref[i] = w
        for place, send in zip(at, sends):

            @pl.when(place < send.shape[0])
            def _(place=place, send=send):
                send[place] = w

    each(w_ref.shape[0], one)


def combine(places, mine, other, diag, came, most_columns):
    slab, most, block = diag.shape[0], came[0].shape[0], diag.shape[1:]
    chips = len(came) + 1
    sizes = [slab] + [most] * (chips - 1) + [most_columns] * (places.shape[0] - chips + 1)
    whole = lambda n: pl.BlockSpec((n,) + block, lambda i, s: (0, 0, 0))
    own, *sends = pl.pallas_call(
        functools.partial(combine_kernel, chips),
        grid_spec=pltpu.PrefetchScalarGridSpec(
            num_scalar_prefetch=1,
            grid=(1,),
            in_specs=[whole(slab)] * 3 + [whole(most)] * (chips - 1),
            out_specs=[whole(n) for n in sizes],
        ),
        out_shape=[jax.ShapeDtypeStruct((n,) + block, jnp.float32) for n in sizes],
        compiler_params=params(*[(2 * n,) + block for n in sizes], *[(2 * slab,) + block] * 3, *[(2 * most,) + block] * chips),
        name="combine",
    )(places, mine, other, diag, *came)
    return own, sends[: chips - 1], sends[chips - 1 :]


def together(*values):
    return lax.optimization_barrier(values)


def flip_row(part, bit):
    return lax.ppermute(part, "row", [(i, i ^ bit) for i in range(lax.axis_size("row"))])


def from_row(v, d, back=False):
    rows = lax.axis_size("row")
    if rows == 4:
        return flip_row(v, d)
    pairs = [((i + d) % rows, i) for i in range(rows)]
    return lax.ppermute(v, "row", [pair[::-1] for pair in pairs] if back else pairs)


def columns_first(v):
    rows = lax.axis_size("row")
    return [from_row(v, d) for d in range(1, 3 if rows == 4 else rows)]


def columns_second(first):
    if lax.axis_size("row") != 4:
        return []
    middle = first[0].shape[0] // 2
    return [flip_row(first[0][:middle], 2), flip_row(first[1][middle:], 1)]


def column_place(group, own, rows):
    return group ^ own if rows == 4 else (group - own) % rows


def swap_cores(v):
    return lax.ppermute(v, "col", [(i, i ^ 1) for i in range(lax.axis_size("col"))])


def pass_on(v, up, sources):
    move = CORES if up else -CORES
    return lax.ppermute(v, "col", [(z * CORES + c, z * CORES + c + move) for z in sources for c in range(CORES)])


def hop_both(up, down, hop, chips):
    return (
        pass_on(up, True, range(hop - 1, chips - 1)),
        pass_on(down, False, range(1, chips - hop + 1)),
    )


def row_parts(own, ups, downs, most):
    slab, chips = own[0].shape[0], len(ups) + 1
    half = slab + (chips - 1) * most
    parts, choices = [], []
    for side in range(CORES):
        parts.append(own[side])
        choices.append((side * half, None))
        for distance in range(1, chips):
            start = side * half + slab
            parts.append(downs[distance - 1][side])
            choices.append((start + (distance - 1) * most, (chips - distance, True)))
            parts.append(ups[distance - 1][side])
            choices.append((start + (chips - distance - 1) * most, (distance, False)))
    return parts, tuple(choices)


def ring_parts(own, came, most):
    slab, chips = own[0].shape[0], len(came) + 1
    half = slab + (chips - 1) * most
    parts, choices = [], []
    for side in range(CORES):
        parts.append(own[side])
        choices.append((side * half, None))
        for r in range(1, chips):
            parts.append(came[r - 1][side])
            choices.append((side * half + slab + (chips - r - 1) * most, None))
    return parts, tuple(choices)


def round_ring(v, r, chips):
    pairs = [(z * CORES + c, (z + r) % chips * CORES + c) for z in range(chips) for c in range(CORES)]
    return lax.ppermute(v, "col", pairs)


def line_pattern(wanted, chip):
    chips = lax.axis_size("col") // CORES
    wanted = jnp.maximum(wanted, swap_cores(wanted))
    table = jnp.where(jnp.arange(chips)[:, None] == chip, wanted[None], 0)
    steps = chips.bit_length() - 1 if chips & (chips - 1) == 0 else chips - 1
    for step in range(steps):
        there = (lambda z: z ^ 1 << step) if steps < chips - 1 else (lambda z: (z + 1) % chips)
        pairs = [(z * CORES + c, there(z) * CORES + c) for z in range(chips) for c in range(CORES)]
        table = jnp.maximum(table, lax.ppermute(table, "col", pairs))
    return wanted, table


def places_in_lists(wanted, slab):
    before = jnp.arange(slab)[:, None] > jnp.arange(slab)[None, :]
    place = jnp.sum(jnp.where(before, wanted[..., None, :], 0), axis=-1)
    return jnp.where(wanted > 0, place, slab)


def longest_list(table, slab):
    chips = table.shape[0]
    counts = jnp.sum(table.reshape(chips, -1, slab), axis=2)
    own = jnp.arange(chips)[:, None] == jnp.arange(counts.shape[1])[None, :] // CORES
    return jnp.max(jnp.where(own, 0, counts))


def place_of(listed, relative, inner, side, live, slab, chips, most):
    inside = jnp.where(relative == 0, inner, slab + (relative - 1) * most + listed)
    return jnp.where(live, side * (slab + (chips - 1) * most) + inside, 0)


def both_cores(flow):
    return [(part, swap_cores(part)) for part in flow]


def iterate(most, most_columns, stride, slab, chips, scalars, places, samples, blocks, p_diag, col_x, x_own, x_ups, x_downs, p_mine, other):
    half = slab + (chips - 1) * most
    row_x = None
    for iteration in range(ITERS):
        last = iteration == ITERS - 1
        if iteration > 0:
            other = swap_cores(p_other)
        came = []
        for r in range(1, chips):
            at = slab + (r - 1) * stride
            came.append(round_ring(p_mine[at : at + most] + other[at : at + most], r, chips))
        if row_x is None:
            came, flow = together(came, hop_both(x_ups[-1], x_downs[-1], chips - 1, chips))
            x_ups, x_downs = x_ups + [flow[0]], x_downs + [flow[1]]
        own_w, sends, column_sends = combine(places, p_mine, other, p_diag, together(*came), most_columns)
        came = [round_ring(send, r, chips) for r, send in enumerate(sends, 1)]
        w_columns = [from_row(send, d) for d, send in enumerate(column_sends, 1)]
        w_own = (own_w, swap_cores(own_w))
        updated = diag_update(samples, own_w, blocks, last)
        rest, w_columns, updated = together(came[:-1], w_columns, updated)
        if row_x is None:
            row_x = row_parts(x_own, both_cores(x_ups), both_cores(x_downs), slab)
        came = both_cores(rest) + both_cores(came[-1:])
        row_w = ring_parts(w_own, came, most)
        state = ([own_w] + w_columns, row_x, row_w, updated[0])
        result = off_slots(scalars, col_x, blocks, slab, half, state, not last)
        blocks = result[0]
        if not last:
            p_diag, (p_mine, p_other), stride = updated[1], result[1:], most
    return blocks


def shards(samples, omega, block_rows, block_cols):
    n_row, n_col = lax.axis_size("row"), lax.axis_size("col")
    a, b = lax.axis_index("row"), lax.axis_index("col")
    slab = samples.shape[0]
    chips = n_col // CORES
    chip, core = b // CORES, b % CORES
    blocks = omega[0, 0]
    rows = block_rows[0, 0, slab:]
    cols = block_cols[0, 0, slab:]

    first = columns_first(samples)
    x_own = (samples, swap_cores(samples))
    x_ups, x_downs = ([part] for part in hop_both(samples, samples, 1, chips))

    live = rows >= 0
    local = rows - a * (slab * n_col)
    owner, inner = local // slab, local % slab
    side = (owner % CORES) ^ core
    relative = (owner // CORES - chip) % chips
    group, column_inner = column_place(cols // slab // n_col, a, n_row), cols % slab
    column = jnp.where(live, group * slab + column_inner, 0)

    p_diag = diag_products(samples, blocks)
    among = lambda ids, count: jnp.any((ids[:, None] == jnp.arange(count)[None, :]) & live[:, None], axis=0).astype(jnp.int32)
    columns = among(column, n_row * slab).reshape(n_row, slab)
    longest_columns = jnp.max(jnp.sum(columns[1:], axis=1))
    wanted, table = line_pattern(jnp.concatenate([among(local, n_col * slab), longest_columns[None]]), chip)
    x_ups, x_downs, table, first, p_diag = together(x_ups, x_downs, table, first, p_diag)
    for hop in range(2, chips - 1):
        up, down = hop_both(x_ups[-1], x_downs[-1], hop, chips)
        x_ups, x_downs = x_ups + [up], x_downs + [down]
    col_x = [samples] + first + columns_second(first)
    longest_columns = jnp.max(table[:, -1])
    longest = longest_list(table[:, :-1], slab)
    told = [from_row(jnp.concatenate([columns[d], longest[None], longest_columns[None]]), d, True) for d in range(1, n_row)]
    longest, longest_columns = functools.reduce(jnp.maximum, [each[slab:] for each in told], jnp.stack([longest, longest_columns]))
    mine = lax.dynamic_slice_in_dim(table, b * slab, slab, 1)
    ahead = jnp.arange(chips)[None, :] == (chip + jnp.arange(1, chips)[:, None]) % chips
    lists = list(jnp.sum(jnp.where(ahead[:, :, None], mine[None], 0), axis=1)) + [each[:slab] for each in told]
    places = places_in_lists(jnp.stack(lists), slab).astype(jnp.int32)

    pick = lambda table, ids: jnp.sum(jnp.where(ids[:, None] == jnp.arange(table.size)[None, :], table.reshape(1, -1), 0), axis=1)
    listed = pick(places_in_lists(wanted[:-1].reshape(-1, slab), slab), local)
    column_listed = pick(places_in_lists(columns, slab), column)
    place = lambda inner_place, most: place_of(inner_place, relative, inner, side, live, slab, chips, most)
    x_place = place(inner, slab)

    def scalars_of(most, most_columns):
        half = slab + (chips - 1) * most
        at = place(listed, most)
        target = jnp.where(live, at, CORES * half)
        w_column = jnp.where(group == 0, column_inner, slab + (group - 1) * most_columns + column_listed)
        w_column = jnp.where(live, w_column, 0)
        rows = [target, column, at, jnp.full_like(at, chip), live, x_place, w_column]
        return jnp.stack([row.astype(jnp.int32) for row in rows])

    def branch(most):
        most_columns = slab if most == slab else min(slab, MOST_COLUMNS)

        def run(*state):
            scalars = scalars_of(most, most_columns)
            return iterate(most, most_columns, slab, slab, chips, scalars, places, *state)

        return run

    tiers = sorted({min(tier, slab) for tier in TIERS})
    longest = jnp.where(longest_columns > MOST_COLUMNS, slab, longest)
    scalars = scalars_of(slab, slab)
    x_ups, x_downs, col_x, longest, scalars = together(x_ups, x_downs, col_x, longest, scalars)
    p_mine, p_other = off_slots(scalars, col_x, blocks, slab, slab * chips)
    state = (samples, blocks, p_diag, col_x, x_own, x_ups, x_downs, p_mine, swap_cores(p_other))

    def choose(tiers, longest, state):
        if len(tiers) == 1:
            return branch(tiers[0])(*state)
        middle = len(tiers) // 2
        return lax.cond(
            longest <= tiers[middle - 1],
            lambda state: choose(tiers[:middle], longest, state),
            lambda state: choose(tiers[middle:], longest, state),
            state,
        )

    return choose(tiers, longest, state)[None, None]


def solution(mesh):
    return jax.shard_map(
        shards,
        mesh=mesh,
        in_specs=(
            P(("row", "col"), None, None),
            P("row", "col", None, None, None),
            P("row", "col", None),
            P("row", "col", None),
        ),
        out_specs=P("row", "col", None, None, None),
        check_vma=False,
    )
```

```python
import functools
import math

import jax
import jax.numpy as jnp
from jax import lax
from jax.experimental import pallas as pl
from jax.experimental.pallas import tpu as pltpu
from jax.sharding import PartitionSpec as P

ITERS = 2
STEP = 0.5
PENALTY = 0.1
VMEM_SPARE = 20 * 1024 * 1024
CORES = 2
UNROLL = 8
TIERS = (15, 17, 19, 1 << 30)
MOST_COLUMNS = 24


def split(x):
    high = x.astype(jnp.bfloat16)
    low = (x - high.astype(jnp.float32)).astype(jnp.bfloat16)
    return high, low


def dot(a, b, dims):
    return lax.dot_general(a, b, (dims, ((), ())), preferred_element_type=jnp.float32)


def product(x, block):
    x_high, x_low = split(x)
    o_high, o_low = split(block)
    count = x.shape[0]
    dims = ((1,), (1,))
    both = dot(o_high, jnp.concatenate([x_high, x_low], 0), dims)
    return (both[:, :count] + both[:, count:] + dot(o_low, x_high, dims)).T


def gradient(left_w, right_x, left_x, right_w):
    a_high, a_low = split(jnp.concatenate([left_w, left_x], 0))
    b_high, b_low = split(jnp.concatenate([right_x, right_w], 0))
    dims = ((0,), (0,))
    return dot(a_high, b_high, dims) + dot(a_low, b_high, dims) + dot(a_high, b_low, dims)


def shrink(v):
    level = STEP * PENALTY
    return v - jnp.clip(v, -level, level)


def lift_diagonal(v, shrunk):
    rows = lax.broadcasted_iota(jnp.int32, v.shape, 0)
    cols = lax.broadcasted_iota(jnp.int32, v.shape, 1)
    eye = rows == cols
    entries = jnp.sum(jnp.where(eye, v, 0.0), axis=0, keepdims=True)
    lifted = 0.5 * (entries + jnp.sqrt(entries * entries + 4.0 * STEP))
    return jnp.where(eye, lifted, shrunk)


def block_count(*sizes):
    for count in (16, 8, 4, 2):
        if all(size % count == 0 for size in sizes):
            return count
    return 1


def each(count, one):
    unroll = UNROLL if count % UNROLL == 0 else 1

    def some(i, carry):
        for j in range(unroll):
            one(i * unroll + j)
        return carry

    lax.fori_loop(0, count // unroll, some, 0)


def diag_products_kernel(x_ref, omega_ref, p_ref):
    def one(k):
        p_ref[k] = product(x_ref[k], omega_ref[k])

    each(x_ref.shape[0], one)


def diag_update_kernel(scale, last, x_ref, w_ref, omega_ref, out_ref, *p_refs):
    def one(k):
        x, w = x_ref[k], w_ref[k]
        v = omega_ref[k] - STEP * (gradient(w, x, x, w) * scale)
        new = lift_diagonal(v, shrink(v))
        out_ref[k] = new
        if not last:
            p_refs[0][k] = product(x, new)

    each(x_ref.shape[0], one)


def params(*shapes):
    held = sum(4 * math.prod(shape) for shape in shapes)
    return pltpu.CompilerParams(vmem_limit_bytes=held + VMEM_SPARE)


def cost(slots, dims, passes, extra=0):
    count, width = dims
    return pl.CostEstimate(
        flops=2 * slots * passes * count * width * width,
        bytes_accessed=slots * (2 * width * width + 4 * count * width) * 4 + extra,
        transcendentals=0,
    )


def diag_products(x, omega):
    slab, count, width = x.shape
    size = block_count(slab)
    x_spec = pl.BlockSpec((size, count, width), lambda i: (i, 0, 0))
    o_spec = pl.BlockSpec((size, width, width), lambda i: (i, 0, 0))
    return pl.pallas_call(
        diag_products_kernel,
        grid=(slab // size,),
        in_specs=[x_spec, o_spec],
        out_specs=x_spec,
        out_shape=jax.ShapeDtypeStruct(x.shape, jnp.float32),
        compiler_params=params(*[(2 * size, count, width)] * 2, (2 * size, width, width)),
        cost_estimate=cost(slab, (count, width), 3),
        name="diag_products",
    )(x, omega)


def diag_update(x, w, omega, last):
    slab, count, width = x.shape
    size = block_count(slab)
    x_spec = pl.BlockSpec((size, count, width), lambda i: (i, 0, 0))
    o_spec = pl.BlockSpec((size, width, width), lambda i: (i, 0, 0))
    outs = [jax.ShapeDtypeStruct(omega.shape, jnp.float32)]
    specs = [o_spec]
    if not last:
        outs.append(jax.ShapeDtypeStruct(x.shape, jnp.float32))
        specs.append(x_spec)
    return pl.pallas_call(
        functools.partial(diag_update_kernel, 0.5 / count, last),
        grid=(slab // size,),
        in_specs=[x_spec, x_spec, o_spec],
        out_specs=specs,
        out_shape=outs,
        compiler_params=params(*[(2 * size, count, width)] * 3, *[(2 * size, width, width)] * 2),
        cost_estimate=cost(slab, (count, width), 9),
        name="diag_update",
    )(x, w, omega)


def off_kernel(plan, scalars, *refs):
    update, products, scale, size, n_col, n_col_w, x_choices, w_choices = plan
    steps = pl.num_programs(0)
    step = pl.program_id(0)
    refs = list(refs)
    take = lambda n: [refs.pop(0) for _ in range(n)]
    col_x_parts = take(n_col)
    col_w_parts = take(n_col_w)
    row_x_parts = take(len(x_choices)) if update else []
    row_w_parts = take(len(w_choices)) if update else []
    if update:
        take(1)
    (omega_ref,) = take(1)
    out_refs = take(1) if update else []
    p_refs = take(2) if products else []
    col_x = take(1)[0]
    col_w, row_x, row_w = take(3) if update else (None, None, None)
    acc = take(1)[0] if products else None
    (sems,) = take(1)
    (p_sems,) = take(1) if products else (None,)
    z_index = scalars[3, 0]

    copies = []

    def add(condition, source, target):
        copies.append((condition, pltpu.make_async_copy(source, target, sems.at[len(copies)])))

    def columns(parts, target):
        at = 0
        for part in parts:
            add(None, part, target.at[pl.ds(at, part.shape[0])])
            at += part.shape[0]

    def rows(parts, choices, target):
        for part, (at, wanted) in zip(parts, choices):
            condition = None
            if wanted is not None:
                bound, above = wanted
                condition = z_index < bound if above else z_index >= bound
            add(condition, part, target.at[pl.ds(at, part.shape[0])])

    columns(col_x_parts, col_x)
    if update:
        columns(col_w_parts, col_w)
        rows(row_x_parts, x_choices, row_x)
        rows(row_w_parts, w_choices, row_w)

    def for_all(action):
        for condition, copy in copies:
            if condition is None:
                action(copy)
            else:
                pl.when(condition)(functools.partial(action, copy))

    @pl.when(step == 0)
    def _():
        for_all(lambda copy: copy.start())
        if products:
            acc[...] = jnp.zeros_like(acc)
        for_all(lambda copy: copy.wait())

    def one_slot(k):
        slot = step * size + k
        target = scalars[0, slot]
        column = scalars[1, slot]
        x = col_x[column]
        block = omega_ref[k]
        if update:
            row_at, x_at = scalars[2, slot], scalars[5, slot]
            grad = gradient(row_w[row_at], x, row_x[x_at], col_w[scalars[6, slot]]) * scale
            block = jnp.where(scalars[4, slot] > 0, shrink(block - STEP * grad), 0.0)
            out_refs[0][k] = block
        if products:
            acc[target] += product(x, block)

    each(size, one_slot)

    if products:

        @pl.when(step == steps - 1)
        def _():
            half = p_refs[0].shape[0]
            outs = [
                pltpu.make_async_copy(acc.at[pl.ds(side * half, half)], p_refs[side], p_sems.at[side])
                for side in range(2)
            ]
            for copy in outs:
                copy.start()
            for copy in outs:
                copy.wait()


def off_slots(scalars, col_x, omega, slab, half, state=None, products=True):
    update = state is not None
    cap, width = omega.shape[0], omega.shape[1]
    count = col_x[0].shape[1]
    off = cap - slab
    size = block_count(slab, off)
    any_spec = pl.BlockSpec(memory_space=pl.ANY)
    slots = pl.BlockSpec((size, width, width), lambda i, s: (slab // size + i, 0, 0))
    col_blocks = sum(part.shape[0] for part in col_x)
    block = (count, width)
    operands = list(col_x)
    scratch = [pltpu.VMEM((col_blocks,) + block, jnp.float32)]
    copies = len(col_x)
    col_w, x_choices, w_choices = (), (), ()
    if update:
        col_w, (row_x, x_choices), (row_w, w_choices), buffer = state
        operands += list(col_w) + list(row_x) + list(row_w) + [buffer]
        row_blocks = lambda parts, choices: max(at + part.shape[0] for part, (at, _) in zip(parts, choices))
        scratch += [
            pltpu.VMEM((sum(part.shape[0] for part in col_w),) + block, jnp.float32),
            pltpu.VMEM((row_blocks(row_x, x_choices),) + block, jnp.float32),
            pltpu.VMEM((row_blocks(row_w, w_choices),) + block, jnp.float32),
        ]
        copies = len(col_x) + len(col_w) + len(row_x) + len(row_w)
    in_specs = [any_spec] * len(operands) + [slots]
    aliases = {len(operands): 0} if update else {}
    outs, out_specs = [], []
    if update:
        outs.append(jax.ShapeDtypeStruct(omega.shape, jnp.float32))
        out_specs.append(slots)
    if products:
        outs += [jax.ShapeDtypeStruct((half,) + block, jnp.float32)] * 2
        out_specs += [any_spec] * 2
        scratch.append(pltpu.VMEM((CORES * half + 1,) + block, jnp.float32))
    scratch.append(pltpu.SemaphoreType.DMA((copies,)))
    if products:
        scratch.append(pltpu.SemaphoreType.DMA((2,)))
    held = [(4 * size, width, width)] + [each.shape for each in scratch if each.dtype == jnp.float32]
    plan = (update, products, 0.5 / count, size, len(col_x), len(col_w), x_choices, w_choices)
    return pl.pallas_call(
        functools.partial(off_kernel, plan),
        grid_spec=pltpu.PrefetchScalarGridSpec(
            num_scalar_prefetch=1,
            grid=(off // size,),
            in_specs=in_specs,
            out_specs=out_specs,
            scratch_shapes=scratch,
        ),
        out_shape=outs,
        input_output_aliases=aliases,
        compiler_params=params(*held),
        cost_estimate=cost(off, block, 3 * (2 * update + products), 2 * half * count * width * 4),
        name="off_update" if update else "off_products",
    )(scalars, *operands, omega)


def combine_kernel(chips, places, mine_ref, other_ref, diag_ref, *refs):
    came, (w_ref, *sends) = refs[: chips - 1], refs[chips - 1 :]
    most = came[0].shape[0]
    def one(i):
        at = [places[r, i] for r in range(len(sends))]
        w = mine_ref[i] + other_ref[i] + diag_ref[i]
        for r in range(1, chips):
            place = at[chips - r - 1]
            w = w + jnp.where(place < most, came[r - 1][jnp.minimum(place, most - 1)], 0.0)
        w_ref[i] = w
        for place, send in zip(at, sends):

            @pl.when(place < send.shape[0])
            def _(place=place, send=send):
                send[place] = w

    each(w_ref.shape[0], one)


def combine(places, mine, other, diag, came, most_columns):
    slab, most, block = diag.shape[0], came[0].shape[0], diag.shape[1:]
    chips = len(came) + 1
    sizes = [slab] + [most] * (chips - 1) + [most_columns] * (places.shape[0] - chips + 1)
    whole = lambda n: pl.BlockSpec((n,) + block, lambda i, s: (0, 0, 0))
    own, *sends = pl.pallas_call(
        functools.partial(combine_kernel, chips),
        grid_spec=pltpu.PrefetchScalarGridSpec(
            num_scalar_prefetch=1,
            grid=(1,),
            in_specs=[whole(slab)] * 3 + [whole(most)] * (chips - 1),
            out_specs=[whole(n) for n in sizes],
        ),
        out_shape=[jax.ShapeDtypeStruct((n,) + block, jnp.float32) for n in sizes],
        compiler_params=params(*[(2 * n,) + block for n in sizes], *[(2 * slab,) + block] * 3, *[(2 * most,) + block] * chips),
        name="combine",
    )(places, mine, other, diag, *came)
    return own, sends[: chips - 1], sends[chips - 1 :]


def pack_kernel(places, *refs):
    half = len(refs) // 2

    def one(i):
        for list_, (source, target) in enumerate(zip(refs[:half], refs[half:])):

            @pl.when(places[list_, i] < target.shape[0])
            def _(list_=list_, source=source, target=target):
                target[places[list_, i]] = source[i]

    each(refs[0].shape[0], one)


def pack(places, sources, most):
    slab, block = sources[0].shape[0], sources[0].shape[1:]
    whole = lambda n: pl.BlockSpec((n,) + block, lambda i, s: (0, 0, 0))
    return pl.pallas_call(
        pack_kernel,
        grid_spec=pltpu.PrefetchScalarGridSpec(
            num_scalar_prefetch=1,
            grid=(1,),
            in_specs=[whole(slab)] * len(sources),
            out_specs=[whole(most)] * len(sources),
        ),
        out_shape=[jax.ShapeDtypeStruct((most,) + block, jnp.float32)] * len(sources),
        compiler_params=params(*[(2 * (slab + most),) + block] * len(sources)),
        name="pack",
    )(places, *sources)


def together(*values):
    return lax.optimization_barrier(values)


def flip_row(part, bit):
    return lax.ppermute(part, "row", [(i, i ^ bit) for i in range(lax.axis_size("row"))])


def from_row(v, d, back=False):
    rows = lax.axis_size("row")
    if rows == 4:
        return flip_row(v, d)
    pairs = [((i + d) % rows, i) for i in range(rows)]
    return lax.ppermute(v, "row", [pair[::-1] for pair in pairs] if back else pairs)


def columns_first(v):
    rows = lax.axis_size("row")
    return [from_row(v, d) for d in range(1, 3 if rows == 4 else rows)]


def columns_second(first):
    if lax.axis_size("row") != 4:
        return []
    middle = first[0].shape[0] // 2
    return [flip_row(first[0][:middle], 2), flip_row(first[1][middle:], 1)]


def column_place(group, own, rows):
    return group ^ own if rows == 4 else (group - own) % rows


def swap_cores(v):
    return lax.ppermute(v, "col", [(i, i ^ 1) for i in range(lax.axis_size("col"))])


def pass_on(v, up, sources):
    move = CORES if up else -CORES
    return lax.ppermute(v, "col", [(z * CORES + c, z * CORES + c + move) for z in sources for c in range(CORES)])


def hop_both(up, down, hop, chips):
    return (
        pass_on(up, True, range(hop - 1, chips - 1)),
        pass_on(down, False, range(1, chips - hop + 1)),
    )


def row_parts(own, ups, downs, most):
    slab, chips = own[0].shape[0], len(ups) + 1
    half = slab + (chips - 1) * most
    parts, choices = [], []
    for side in range(CORES):
        parts.append(own[side])
        choices.append((side * half, None))
        for distance in range(1, chips):
            start = side * half + slab
            parts.append(downs[distance - 1][side])
            choices.append((start + (distance - 1) * most, (chips - distance, True)))
            parts.append(ups[distance - 1][side])
            choices.append((start + (chips - distance - 1) * most, (distance, False)))
    return parts, tuple(choices)


def ring_parts(own, came, most):
    slab, chips = own[0].shape[0], len(came) + 1
    half = slab + (chips - 1) * most
    parts, choices = [], []
    for side in range(CORES):
        parts.append(own[side])
        choices.append((side * half, None))
        for r in range(1, chips):
            parts.append(came[r - 1][side])
            choices.append((side * half + slab + (chips - r - 1) * most, None))
    return parts, tuple(choices)


def round_ring(v, r, chips):
    pairs = [(z * CORES + c, (z + r) % chips * CORES + c) for z in range(chips) for c in range(CORES)]
    return lax.ppermute(v, "col", pairs)


def line_pattern(wanted, chip):
    chips = lax.axis_size("col") // CORES
    around = [wanted] + list(together(*[round_ring(wanted, chips - r, chips) for r in range(1, chips)]))
    here = jnp.arange(chips)[:, None] == (chip + jnp.arange(chips)[None, :]) % chips
    return jnp.sum(jnp.where(here[:, :, None], jnp.stack(around)[None], 0), axis=1)


def places_in_lists(wanted, slab):
    before = jnp.arange(slab)[:, None] > jnp.arange(slab)[None, :]
    place = jnp.sum(jnp.where(before, wanted[..., None, :], 0), axis=-1)
    return jnp.where(wanted > 0, place, slab)


def longest_list(table, slab):
    chips = table.shape[0]
    counts = jnp.sum(table.reshape(chips, -1, slab), axis=2)
    own = jnp.arange(chips)[:, None] == jnp.arange(counts.shape[1])[None, :] // CORES
    return jnp.max(jnp.where(own, 0, counts))


def place_of(listed, relative, inner, side, live, slab, chips, most):
    inside = jnp.where(relative == 0, inner, slab + (relative - 1) * most + listed)
    return jnp.where(live, side * (slab + (chips - 1) * most) + inside, 0)


def both_cores(flow):
    return [(part, swap_cores(part)) for part in flow]


def iterate(most, most_columns, stride, slab, chips, scalars, places, far_places, samples, blocks, p_diag, col_x, x_own, x_ups, x_downs, p_mine, other):
    half = slab + (chips - 1) * most
    row_x = None
    for iteration in range(ITERS):
        last = iteration == ITERS - 1
        if iteration > 0:
            other = swap_cores(p_other)
        came = []
        for r in range(1, chips):
            at = slab + (r - 1) * stride
            came.append(round_ring(p_mine[at : at + most] + other[at : at + most], r, chips))
        if row_x is None:
            far = pack(far_places, [x_ups[-1], x_downs[-1]], most)
            came[-1], far = together(came[-1], far)
            came, far = together(came, both_cores(hop_both(*far, chips - 1, chips)))
        own_w, sends, column_sends = combine(places, p_mine, other, p_diag, together(*came), most_columns)
        came = [round_ring(send, r, chips) for r, send in enumerate(sends, 1)]
        w_columns = [from_row(send, d) for d, send in enumerate(column_sends, 1)]
        w_own = (own_w, swap_cores(own_w))
        updated = diag_update(samples, own_w, blocks, last)
        rest, w_columns, updated = together(came[:-1], w_columns, updated)
        if row_x is None:
            row_x = row_parts(x_own, both_cores(x_ups) + far[:1], both_cores(x_downs) + far[1:], slab)
        came = both_cores(rest) + both_cores(came[-1:])
        row_w = ring_parts(w_own, came, most)
        state = ([own_w] + w_columns, row_x, row_w, updated[0])
        result = off_slots(scalars, col_x, blocks, slab, half, state, not last)
        blocks = result[0]
        if not last:
            p_diag, (p_mine, p_other), stride = updated[1], result[1:], most
    return blocks


def shards(samples, omega, block_rows, block_cols):
    n_row, n_col = lax.axis_size("row"), lax.axis_size("col")
    a, b = lax.axis_index("row"), lax.axis_index("col")
    slab = samples.shape[0]
    chips = n_col // CORES
    chip, core = b // CORES, b % CORES
    blocks = omega[0, 0]
    rows = block_rows[0, 0, slab:]
    cols = block_cols[0, 0, slab:]

    first = columns_first(samples)
    x_own = (samples, swap_cores(samples))
    x_ups, x_downs = ([part] for part in hop_both(samples, samples, 1, chips))

    live = rows >= 0
    local = rows - a * (slab * n_col)
    owner, inner = local // slab, local % slab
    side = (owner % CORES) ^ core
    relative = (owner // CORES - chip) % chips
    group, column_inner = column_place(cols // slab // n_col, a, n_row), cols % slab
    column = jnp.where(live, group * slab + column_inner, 0)

    p_diag = diag_products(samples, blocks)
    among = lambda ids, count: jnp.any((ids[:, None] == jnp.arange(count)[None, :]) & live[:, None], axis=0).astype(jnp.int32)
    columns = among(column, n_row * slab).reshape(n_row, slab)
    longest_columns = jnp.max(jnp.sum(columns[1:], axis=1))
    wanted = jnp.concatenate([among(local, n_col * slab), longest_columns[None]])
    wanted, first = together(jnp.maximum(wanted, swap_cores(wanted)), first)
    table = line_pattern(wanted, chip)
    x_ups, x_downs, table, first, p_diag = together(x_ups, x_downs, table, first, p_diag)
    for hop in range(2, chips - 1):
        up, down = hop_both(x_ups[-1], x_downs[-1], hop, chips)
        x_ups, x_downs = x_ups + [up], x_downs + [down]
    col_x = [samples] + first + columns_second(first)
    longest_columns = jnp.max(table[:, -1])
    longest = longest_list(table[:, :-1], slab)
    told = [from_row(jnp.concatenate([columns[d], longest[None], longest_columns[None]]), d, True) for d in range(1, n_row)]
    longest, longest_columns = functools.reduce(jnp.maximum, [each[slab:] for each in told], jnp.stack([longest, longest_columns]))
    mine = lax.dynamic_slice_in_dim(table, b * slab, slab, 1)
    ahead = jnp.arange(chips)[None, :] == (chip + jnp.arange(1, chips)[:, None]) % chips
    lists = list(jnp.sum(jnp.where(ahead[:, :, None], mine[None], 0), axis=1)) + [each[:slab] for each in told]
    places = places_in_lists(jnp.stack(lists), slab).astype(jnp.int32)

    pick = lambda table, ids: jnp.sum(jnp.where(ids[:, None] == jnp.arange(table.size)[None, :], table.reshape(1, -1), 0), axis=1)
    listed = pick(places_in_lists(wanted[:-1].reshape(-1, slab), slab), local)
    column_listed = pick(places_in_lists(columns, slab), column)
    place = lambda inner_place, most: place_of(inner_place, relative, inner, side, live, slab, chips, most)
    far = abs(owner // CORES - chip) == chips - 1
    x_place = place(jnp.where(far, listed, inner), slab)
    far_wanted = [table[chips - 1, : n_col * slab].reshape(-1, slab)[core], table[0, : n_col * slab].reshape(-1, slab)[n_col - CORES + core]]
    far_places = places_in_lists(jnp.stack(far_wanted), slab).astype(jnp.int32)

    def scalars_of(most, most_columns):
        half = slab + (chips - 1) * most
        at = place(listed, most)
        target = jnp.where(live, at, CORES * half)
        w_column = jnp.where(group == 0, column_inner, slab + (group - 1) * most_columns + column_listed)
        w_column = jnp.where(live, w_column, 0)
        rows = [target, column, at, jnp.full_like(at, chip), live, x_place, w_column]
        return jnp.stack([row.astype(jnp.int32) for row in rows])

    def branch(most):
        most_columns = slab if most == slab else min(slab, MOST_COLUMNS)

        def run(*state):
            scalars = scalars_of(most, most_columns)
            return iterate(most, most_columns, slab, slab, chips, scalars, places, far_places, *state)

        return run

    tiers = sorted({min(tier, slab) for tier in TIERS})
    longest = jnp.where(longest_columns > MOST_COLUMNS, slab, longest)
    scalars = scalars_of(slab, slab)
    x_ups, x_downs, col_x, longest, scalars = together(x_ups, x_downs, col_x, longest, scalars)
    p_mine, p_other = off_slots(scalars, col_x, blocks, slab, slab * chips)
    state = (samples, blocks, p_diag, col_x, x_own, x_ups, x_downs, p_mine, swap_cores(p_other))

    def choose(tiers, longest, state):
        if len(tiers) == 1:
            return branch(tiers[0])(*state)
        middle = len(tiers) // 2
        return lax.cond(
            longest <= tiers[middle - 1],
            lambda state: choose(tiers[:middle], longest, state),
            lambda state: choose(tiers[middle:], longest, state),
            state,
        )

    return choose(tiers, longest, state)[None, None]


def solution(mesh):
    return jax.shard_map(
        shards,
        mesh=mesh,
        in_specs=(
            P(("row", "col"), None, None),
            P("row", "col", None, None, None),
            P("row", "col", None),
            P("row", "col", None),
        ),
        out_specs=P("row", "col", None, None, None),
        check_vma=False,
    )
```
